512 devices in a mesh: replica: 32 (over z_lo, y, core), fsdp: 16 (over z_hi, x).
Axes of the slice: x: 4, y: 4, z: 16 (z_hi: 4, z_lo: 4; z = z_hi * 4 + z_lo), core: 2. Of those that a mesh axis runs over, the one named last changes fastest.
Arguments:
- activations: bfloat16 [32, 2048, 256], P('replica', 'fsdp'), may hold values from -6 to 6
- cotangent: bfloat16 [32, 2048, 4096], P('replica', 'fsdp'), may hold values from -0.125 to 0.125
- momentum: float32 [32, 256, 4096], P('replica', 'fsdp'), may hold values from -6 to 6
- kept_index: int32 [8], replicated, may hold values from 0 to 63, as said below
Outputs:
- update: bfloat16 [256, 4096], P('fsdp')
- momentum_out: float32 [32, 256, 4096], P('replica', 'fsdp')
The draws below stay inside these ranges and needn't reach their ends.
Inputs may be any that keep to these rules, and one draw needn't show every extreme that they name: `kept_index`: 8 different numbers; 0 and 63 are always among them.
All inputs are finite; a program needn't handle non-finite values.
Results may differ from the reference program's by a relative error of at most 0.00085.
Values may be sent and summed in bfloat16 or wider, within the bound.
A program may use at most 192 MiB of HBM per device.

```python
import math
import jax
import jax.numpy as jnp
from jax import lax

D = 4096
ROWS = 256
TOK_DEV = 128
K = 8
REPLICAS = 32
TOKENS = 2048
N_FSDP = 16


def draw_kept_index(key, part):
    key = jax.random.fold_in(key, 5)
    middle = jax.random.permutation(key, 62)[:K - 2].astype(jnp.int32) + 1
    return jnp.concatenate([jnp.zeros((1,), jnp.int32), middle, jnp.full((1,), 63, jnp.int32)]).astype(jnp.int32)


def spiked(drawn, key, source, target, parts, factor):
    def block_of(axis_at):
        return (jnp.arange(drawn.shape[axis_at]) // (drawn.shape[axis_at] // parts)).reshape((-1,) + (1,) * (drawn.ndim - 1 - axis_at))

    first = jax.random.permutation(key, parts)[block_of(target)]
    second = (block_of(target) + parts // 2) % parts
    return jnp.where((block_of(source) == first) | (block_of(source) == second), factor * drawn, drawn)


def shard_levels(own_key, dims, pieces, smallest, top_value):
    level, own = 1.0, jax.random.fold_in(own_key, 6)
    for dim, parts in pieces:
        heights = jnp.exp(jax.random.uniform(jax.random.fold_in(own, dim), (parts,), jnp.float32, smallest / len(pieces), top_value / len(pieces)))
        level = level * jnp.repeat(heights, dims[dim] // parts).reshape([-1 if axis == dim else 1 for axis in range(len(dims))])
    return level


def centred(rng, dims, deviation, limit, split=(), kind=jnp.bfloat16):
    drawn = deviation * jax.random.normal(rng, dims, jnp.float32)
    if split:
        drawn = drawn * shard_levels(rng, dims, split, -0.22, 0.18)
    return jnp.clip(drawn, -limit, limit).astype(kind)


def heavy_noise(stream_key, extent, deviation, bound, shards, heavy, held_as=jnp.bfloat16):
    drawn = deviation * jax.random.normal(stream_key, extent, jnp.float32)
    if shards:
        drawn = drawn * shard_levels(stream_key, extent, shards, -0.22, 0.18)
    return jnp.clip(spiked(drawn, jax.random.fold_in(stream_key, 3), *heavy), -bound, bound).astype(held_as)


def setup_inputs(seed: int = 0) -> dict:
    key_of = jax.random.split(jax.random.key(seed), 5)
    return {
        "activations": heavy_noise(key_of[0], (REPLICAS, TOKENS, ROWS), 1.0, 6.0, ((0, 32), (1, 16)), (1, 2, 16, 2.0)),
        "cotangent": centred(key_of[1], (REPLICAS, TOKENS, D), TOKENS ** -0.5, 0.125, ((0, 32), (1, 16))),
        "momentum": centred(key_of[2], (REPLICAS, ROWS, D), 1.0, 6.0, ((0, 32), (1, 16)), jnp.float32),
        "kept_index": draw_kept_index(jax.random.fold_in(key_of[4], 71), 0),
    }


decay_rate = 0.999

def group_basis(kept_index):
    sample_pos = jnp.arange(8, dtype=jnp.float32)
    frequency = jnp.arange(8, dtype=jnp.float32)
    weights = jnp.where(frequency == 0.0, math.sqrt(1.0 / 8.0), 0.5)
    cosine = jnp.cos(math.pi * (2.0 * sample_pos[None, :] + 1.0) * frequency[:, None] / 16.0) * weights[:, None]
    full_table = (cosine[:, None, :, None] * cosine[None, :, None, :]).reshape(64, 8, 8)
    selector = (kept_index[:, None] == jnp.arange(64, dtype=jnp.int32)[None, :]).astype(jnp.float32)
    return jnp.einsum('kc,cij->kij', selector, full_table, precision=lax.Precision.HIGHEST)

def encode_blocks(values_grid, basis_table):
    rows_all, width = values_grid.shape
    blocks = values_grid.reshape(rows_all // 8, 8, width // 8, 8)
    return jnp.einsum('kij,aibj->kab', basis_table, blocks, precision=lax.Precision.HIGHEST)

def decode_blocks(coeffs, basis_table):
    return jnp.einsum('kij,kab->aibj', basis_table, coeffs, precision=lax.Precision.HIGHEST)

def soft_sign(blocks):
    group_scale = jnp.sqrt(lax.optimization_barrier(jnp.mean(blocks * blocks, axis=(1, 3), keepdims=True)) + 1e-06)
    return jnp.tanh(blocks / group_scale)

def reference(activations, cotangent, momentum, kept_index):
    basis_table = group_basis(kept_index)

    def one_replica(operands):
        inputs_one, cotan_one, moment_one = operands
        inputs_f = inputs_one.reshape(N_FSDP, TOK_DEV, ROWS).astype(jnp.float32)
        cotan_f = cotan_one.reshape(N_FSDP, TOK_DEV, D).astype(jnp.float32)
        partials = jnp.einsum('ftr,ftd->frd', inputs_f, cotan_f, precision=lax.Precision.HIGHEST)
        gradient = lax.optimization_barrier(jnp.sum(partials, axis=0))
        accrued = decay_rate * moment_one + gradient
        coeffs = encode_blocks(accrued, basis_table)
        removed = decode_blocks(coeffs, basis_table).reshape(ROWS, D)
        return (coeffs, accrued - removed)
    coeff_all, momentum_out = lax.map(one_replica, (activations, cotangent, momentum))
    total = lax.optimization_barrier(jnp.sum(coeff_all, axis=0))
    decoded = decode_blocks(total, basis_table)
    update = soft_sign(decoded).reshape(ROWS, D).astype(jnp.bfloat16)
    return (update, momentum_out)
```

```python
import functools
import math

import jax
import jax.numpy as jnp
import numpy as np
from jax import lax
from jax.experimental import pallas as pl
from jax.experimental.pallas import tpu as pltpu
from jax.sharding import PartitionSpec as P

MESH = pl.DeviceIdType.MESH
decay_rate = 0.999
f32, bf16 = jnp.float32, jnp.bfloat16
HIGHEST = lax.Precision.HIGHEST


def cosine_table():
    u, i = np.arange(8)[:, None], np.arange(128)[None, :] % 8
    weight = np.where(u == 0, math.sqrt(1.0 / 8.0), 0.5)
    return (weight * np.cos(math.pi * (2 * i + 1) * u / 16)).astype(np.float32)


def halves(value):
    high = value.astype(bf16)
    return high, (value - high.astype(f32)).astype(bf16)


def dot(a, b):
    return jnp.dot(a, b, preferred_element_type=f32)


def wait_bytes(ref, sem):
    pltpu.make_async_copy(ref, ref, sem).wait()


def kernel(kept, table, act, cot, mom, upd, mo, a_in, c_in, m_in, lhs, us, ur, q, qr, s2, s3, upd_v, mo_v,
           local_sem, out_sem, xs, xr, us_s, us_r, q_s, q_r, s2_s, s2_r, s3_s, s3_r):
    r, f = lax.axis_index("replica"), lax.axis_index("fsdp")
    zl, yc, h, x = r // 8, r % 8, f // 4, f % 4
    own_rows = pl.ds(pl.multiple_of(x * 128, 128), 128)
    local = [
        pltpu.make_async_copy(act, a_in.at[own_rows], local_sem.at[0]),
        pltpu.make_async_copy(cot.at[:, pl.ds(pl.multiple_of(x * 1024, 1024), 1024)], c_in.at[own_rows], local_sem.at[1]),
        pltpu.make_async_copy(mom, m_in, local_sem.at[2]),
    ]
    for copy in local:
        copy.start()

    barrier = pltpu.get_barrier_semaphore()

    def greet(who):
        pl.semaphore_signal(barrier, inc=1, device_id=who, device_id_type=MESH)

    fsdp_peer = lambda d: (r, (f + d) % 16)
    yc_peer = lambda d: (zl * 8 + (yc + d) % 8, f)
    z_peer = lambda d: (((zl + d) % 4) * 8 + yc, f)

    @pl.loop(1, 16)
    def _(d):
        greet(fsdp_peer(d))

    @pl.loop(1, 8)
    def _(d):
        greet(yc_peer(d))

    @pl.loop(1, 4)
    def _(d):
        greet(z_peer(d))

    pl.semaphore_wait(barrier, 25)

    def send(src, dst, ssem, rsem, who):
        pltpu.make_async_remote_copy(
            src_ref=src, dst_ref=dst, send_sem=ssem, recv_sem=rsem, device_id=who, device_id_type=MESH
        ).start()

    for d in (2, 1, 3):
        send(act, a_in.at[own_rows], xs.at[0], xr.at[0], (r, h * 4 + (x + d) % 4))
    for c in range(2):
        for d in (2, 1, 3):
            xt = (x + d) % 4
            columns = pl.ds(pl.multiple_of(xt * 1024 + 512 * c, 512), 512)
            send(cot.at[:, columns], c_in.at[own_rows, pl.ds(512 * c, 512)], xs.at[1 + c], xr.at[1 + c], (r, h * 4 + xt))

    k_at = lax.broadcasted_iota(jnp.int32, (8, 128), 0)
    number = jnp.zeros((8, 128), jnp.int32)
    for k in range(8):
        number = jnp.where(k_at == k, kept[k], number)
    row_freq, col_freq = number >> 3, number & 7
    cu = jnp.zeros((8, 128), f32)
    cv = jnp.zeros((8, 128), f32)
    for u in range(8):
        line = jnp.broadcast_to(table[u:u + 1, :], (8, 128))
        cu = jnp.where(row_freq == u, line, cu)
        cv = jnp.where(col_freq == u, line, cv)
    cv512 = jnp.concatenate([cv] * 4, axis=1)
    row_at = lax.broadcasted_iota(jnp.int32, (256, 256), 0)
    col_at = lax.broadcasted_iota(jnp.int32, (256, 256), 1)
    row_block = ((row_at >> 3) & 15) * 2 + (row_at >> 7)
    cu_tall = jnp.concatenate([jnp.concatenate([cu] * 2, axis=1)] * 32, axis=0)
    left = jnp.where((col_at >> 3) == row_block, cu_tall, 0.0)
    at0 = lax.broadcasted_iota(jnp.int32, (512, 128), 0) >> 3
    at1 = lax.broadcasted_iota(jnp.int32, (512, 128), 1)
    gather = [(at0 + 64 * p == at1).astype(bf16) for p in range(2)]
    to0 = lax.broadcasted_iota(jnp.int32, (128, 512), 0)
    to1 = lax.broadcasted_iota(jnp.int32, (128, 512), 1) >> 3
    spread = [(to1 + 64 * p == to0).astype(bf16) for p in range(2)]
    sq0 = lax.broadcasted_iota(jnp.int32, (128, 128), 0) >> 3
    sq1 = lax.broadcasted_iota(jnp.int32, (128, 128), 1) >> 3
    cu_square = jnp.where(sq0 == sq1, jnp.concatenate([cu] * 16, axis=0), 0.0)
    encode16, decode64 = cu_square[:16, :16], cu_square.T[:64, :64]

    def fold(even, odd):
        total = None
        for value, matrix in ((even, gather[0]), (odd, gather[1])):
            for part in halves(value):
                term = dot(part, matrix)
                total = term if total is None else total + term
        return total

    def decode(coeffs):
        out = []
        for p in range(2):
            wide = sum(dot(part, spread[p]) for part in halves(coeffs))
            wide = (wide.reshape(8, 8, 512) * cv512[None]).reshape(64, 512)
            out.append(jnp.dot(decode64, wide, precision=HIGHEST, preferred_element_type=f32))
        return out

    local[2].wait()
    mixed = jnp.dot(encode16, m_in[...], precision=HIGHEST, preferred_element_type=f32)
    mixed = (decay_rate * mixed).reshape(2, 8, 4096)
    strips = [
        jnp.concatenate([mixed[p, :, 512 * j:512 * (j + 1)] * cv512 for j in range(8)], axis=0) for p in range(2)
    ]
    mom_coeffs = fold(*strips)

    local[0].wait()
    wait_bytes(a_in.at[0:384], xr.at[0])
    act_t = a_in[...].astype(f32).T.astype(bf16)
    left_high = left.astype(bf16)
    left_rest = left - left_high.astype(f32)
    left_mid, left_low = halves(left_rest)
    mixed_act = dot(left_high, act_t) + dot(left_mid, act_t) + dot(left_low, act_t)
    high, low = halves(mixed_act)
    lhs[0:256] = act_t
    lhs[256:512] = high
    lhs[512:768] = low

    local[1].wait()
    for c in range(2):
        wait_bytes(c_in.at[0:384, 0:512], xr.at[1 + c])
        block = c_in[:, 512 * c:512 * (c + 1)]
        mix = dot(lhs[256:512], block) + dot(lhs[512:768], block)
        mix = (mix.reshape(32, 8, 512) * cv512[None]).reshape(256, 512)
        us[c, :, 0:8, :] = fold(mix[:128], mix[128:]).reshape(16, 8, 128)
        grad = dot(lhs[0:256], block).reshape(16, 2, 8, 512)
        size = jnp.maximum(jnp.abs(grad[:, 0]), jnp.abs(grad[:, 1]))
        size = functools.reduce(jnp.maximum, [size[:, :, 128 * g:128 * (g + 1)] for g in range(4)])
        size = jnp.maximum(size, 1e-33)
        us[c, :, 8:16, :] = size * (1.0 / 32767.0)

        @pl.loop(1, 16)
        def _(d):
            who = fsdp_peer(d)
            send(us.at[c, who[1]], ur.at[c, f], us_s.at[c], us_r.at[c], who)

        inverse = 32767.0 / size
        inverse = jnp.concatenate([inverse] * 4, axis=2)[:, None]
        q[c] = jnp.round(grad * inverse).astype(jnp.int32).astype(jnp.int16).reshape(16, 16, 512)

        @pl.loop(1, 16)
        def _(d):
            who = fsdp_peer(d)
            send(q.at[c, who[1]], qr.at[c, f], q_s.at[c], q_r.at[c], who)

        ur[c, pl.ds(f, 1)] = us[c, pl.ds(f, 1)]
        qr[c, pl.ds(f, 1)] = q[c, pl.ds(f, 1)]

    for c in range(2):
        wait_bytes(ur.at[c, 0:15], us_r.at[c])
    own = jnp.concatenate(
        [
            ur[c, xx, 0:8, :] + ur[c, 4 + xx, 0:8, :] + ur[c, 8 + xx, 0:8, :] + ur[c, 12 + xx, 0:8, :]
            for xx in range(4)
            for c in range(2)
        ],
        axis=0,
    )
    own = own + mom_coeffs

    s2[pl.ds(yc, 1)] = own[None]

    @pl.loop(1, 8)
    def _(d):
        send(s2.at[yc], s2.at[yc], s2_s, s2_r, yc_peer(d))

    removed = decode(own)
    wait_bytes(s2.at[0:7], s2_r)
    part = functools.reduce(jnp.add, [s2[i] for i in range(8)])
    s3[pl.ds(zl, 1)] = part[None]

    @pl.loop(1, 4)
    def _(d):
        send(s3.at[zl], s3.at[zl], s3_s, s3_r, z_peer(d))

    wait_bytes(s3.at[0:3], s3_r)
    total = s3[0] + s3[1] + s3[2] + s3[3]
    power = jnp.sum((total * total).reshape(8, 8, 128), axis=1, keepdims=True)
    scaled = (total.reshape(8, 8, 128) / jnp.sqrt(power * (1.0 / 64.0) + 1e-06)).reshape(64, 128)
    decoded = decode(scaled)
    for j in range(8):
        block = jnp.concatenate([decoded[p][8 * j:8 * j + 8] for p in range(2)], axis=0)
        upd_v[:, 512 * j:512 * (j + 1)] = jnp.tanh(block).astype(bf16)
    out0 = pltpu.make_async_copy(upd_v, upd, out_sem.at[0])
    out0.start()

    for c in range(2):
        wait_bytes(qr.at[c, 0:15], q_r.at[c])
    for xx in range(4):
        for c in range(2):
            j = 2 * xx + c
            columns = slice(512 * j, 512 * (j + 1))
            grad = None
            for hh in range(4):
                scale = jnp.concatenate([ur[c, 4 * hh + xx, 8:16, :]] * 4, axis=1)
                term = qr[c, 4 * hh + xx].astype(jnp.int32).astype(f32).reshape(2, 8, 512) * scale[None]
                grad = term if grad is None else grad + term
            for p in range(2):
                rows = slice(8 * p, 8 * p + 8)
                mo_v[rows, columns] = decay_rate * m_in[rows, columns] + grad[p] - removed[p][8 * j:8 * j + 8]
    out1 = pltpu.make_async_copy(mo_v, mo, out_sem.at[1])
    out1.start()

    wait_bytes(a_in.at[0:384], xs.at[0])
    for c in range(2):
        wait_bytes(c_in.at[0:384, 0:512], xs.at[1 + c])
        wait_bytes(us.at[c, 0:15], us_s.at[c])
        wait_bytes(q.at[c, 0:15], q_s.at[c])
    wait_bytes(s2.at[0:7], s2_s)
    wait_bytes(s3.at[0:3], s3_s)
    out0.wait()
    out1.wait()


def on_device(activations, cotangent, momentum, kept_index):
    hbm = pl.BlockSpec(memory_space=pl.ANY)
    dma = pltpu.SemaphoreType.DMA
    update, momentum_out = pl.pallas_call(
        kernel,
        name="outer_step",
        out_shape=(jax.ShapeDtypeStruct((16, 4096), bf16), jax.ShapeDtypeStruct((16, 4096), f32)),
        in_specs=[
            pl.BlockSpec(memory_space=pltpu.SMEM),
            pl.BlockSpec(memory_space=pltpu.VMEM),
            hbm,
            hbm,
            hbm,
        ],
        out_specs=(hbm, hbm),
        scratch_shapes=[
            pltpu.VMEM((512, 256), bf16),
            pltpu.VMEM((512, 1024), bf16),
            pltpu.VMEM((16, 4096), f32),
            pltpu.VMEM((768, 512), bf16),
            pltpu.VMEM((2, 16, 16, 128), f32),
            pltpu.VMEM((2, 16, 16, 128), f32),
            pltpu.VMEM((2, 16, 16, 512), jnp.int16),
            pltpu.VMEM((2, 16, 16, 512), jnp.int16),
            pltpu.VMEM((8, 64, 128), f32),
            pltpu.VMEM((4, 64, 128), f32),
            pltpu.VMEM((16, 4096), bf16),
            pltpu.VMEM((16, 4096), f32),
            dma((3,)),
            dma((2,)),
            dma((3,)),
            dma((3,)),
            dma((2,)),
            dma((2,)),
            dma((2,)),
            dma((2,)),
            dma,
            dma,
            dma,
            dma,
        ],
        compiler_params=pltpu.CompilerParams(
            collective_id=1, has_side_effects=True, vmem_limit_bytes=40 * 1024 * 1024
        ),
    )(kept_index, jnp.asarray(cosine_table()), activations[0], cotangent[0], momentum[0])
    return update, momentum_out[None]


def solution(mesh):
    return jax.shard_map(
        on_device,
        mesh=mesh,
        in_specs=(
            P("replica", "fsdp", None),
            P("replica", "fsdp", None),
            P("replica", "fsdp", None),
            P(),
        ),
        out_specs=(P("fsdp", None), P("replica", "fsdp", None)),
        check_vma=False,
    )
```

```python
import functools
import math

import jax
import jax.numpy as jnp
from jax import lax
from jax.experimental import pallas as pl
from jax.experimental.pallas import tpu as pltpu
from jax.sharding import PartitionSpec as P

MESH = pl.DeviceIdType.MESH
decay_rate = 0.999
f32, bf16 = jnp.float32, jnp.bfloat16
HIGHEST = lax.Precision.HIGHEST
WIDTHS = (384, 640)
STARTS = (0, 384)
CHUNKS = range(len(WIDTHS))


def halves(value):
    high = value.astype(bf16)
    return high, (value - high.astype(f32)).astype(bf16)


def dot(a, b):
    return jnp.dot(a, b, preferred_element_type=f32)


def exact(a, b):
    return jnp.dot(a, b, precision=HIGHEST, preferred_element_type=f32)


def iota(shape, dim):
    return lax.broadcasted_iota(jnp.int32, shape, dim)


def wait_bytes(ref, sem):
    pltpu.make_async_copy(ref, ref, sem).wait()


def cosine_table():
    u = iota((8, 128), 0)
    angle = ((2 * (iota((8, 128), 1) & 7) + 1) * u) & 31
    value = jnp.zeros((8, 128), f32)
    for m in range(32):
        value = jnp.where(angle == m, math.cos(math.pi * m / 16), value)
    return jnp.where(u == 0, math.sqrt(1.0 / 8.0), 0.5 * value)


def kernel(kept_hbm, act, cot, mom, upd, mo, kept, a_own, c_own, m_in, a_in, c_in, u1, u1r, u2, u2r, s3, s4,
           q0, q1, qr0, qr1, sc, scr, upd_v, mo_v, local_sem, out_sem, xs, xr, u1_s, u1_r, u2_s, u2_r, s3_s, s3_r,
           s4_s, s4_r, q_s, q_r, sc_s, sc_r, relay):
    q, qr = (q0, q1), (qr0, qr1)
    r, f = lax.axis_index("replica"), lax.axis_index("fsdp")
    zl, yc, h, x = r // 8, r % 8, f // 4, f % 4
    own_rows = pl.ds(pl.multiple_of(x * 128, 128), 128)
    local = [
        pltpu.make_async_copy(kept_hbm, kept, local_sem.at[0]),
        pltpu.make_async_copy(act, a_own, local_sem.at[1]),
        pltpu.make_async_copy(cot, c_own.at[0:128], local_sem.at[2]),
        pltpu.make_async_copy(cot, c_own.at[128:256], local_sem.at[3]),
        pltpu.make_async_copy(mom, m_in, local_sem.at[4]),
        pltpu.make_async_copy(act, a_in.at[own_rows], local_sem.at[5]),
        pltpu.make_async_copy(cot.at[:, pl.ds(pl.multiple_of(x * 1024, 1024), 1024)], c_in.at[own_rows], local_sem.at[6]),
    ]

    def signal(sem, who):
        pl.semaphore_signal(sem, inc=1, device_id=who, device_id_type=MESH)

    def send(src, dst, ssem, rsem, who):
        pltpu.make_async_remote_copy(
            src_ref=src, dst_ref=dst, send_sem=ssem, recv_sem=rsem, device_id=who, device_id_type=MESH
        ).start()

    def fsdp_peer(d):
        return (r, (f + d) % 16)

    def x_peer(d):
        return (r, h * 4 + (x + d) % 4)

    def h_peer(d):
        return (r, ((h + d) % 4) * 4 + x)

    def yc_peer(d):
        return (zl * 8 + (yc + d) % 8, f)

    def z_peer(d):
        return (((zl + d) % 4) * 8 + yc, f)

    barrier = pltpu.get_barrier_semaphore()
    for d in (1, 3):
        signal(barrier, h_peer(d))
    for d in (2, 1, 3):
        signal(barrier, z_peer(d))
        signal(barrier, x_peer(d))

    @pl.loop(1, 8)
    def _(d):
        signal(barrier, yc_peer(d))

    for copy in local:
        copy.start()

    table = cosine_table()
    local[0].wait()
    k_at = iota((8, 128), 0)
    number = jnp.zeros((8, 128), jnp.int32)
    for k in range(8):
        number = jnp.where(k_at == k, kept[k], number)
    row_freq, col_freq = number >> 3, number & 7
    cu = jnp.zeros((8, 128), f32)
    cv = jnp.zeros((8, 128), f32)
    for u in range(8):
        line = jnp.broadcast_to(table[u:u + 1, :], (8, 128))
        cu = jnp.where(row_freq == u, line, cu)
        cv = jnp.where(col_freq == u, line, cv)
    cv512 = jnp.concatenate([cv] * 4, axis=1)
    row_at = iota((256, 256), 0)
    row_block = ((row_at >> 3) & 15) * 2 + (row_at >> 7)
    cu_tall = jnp.concatenate([jnp.concatenate([cu] * 2, axis=1)] * 32, axis=0)
    left = jnp.where((iota((256, 256), 1) >> 3) == row_block, cu_tall, 0.0)
    gather = [((iota((512, 128), 0) >> 3) + 64 * p == iota((512, 128), 1)).astype(bf16) for p in range(2)]
    same = (iota((128, 128), 0) >> 3) == (iota((128, 128), 1) >> 3)
    block_sum = same.astype(bf16)
    cu_square = jnp.where(same, jnp.concatenate([cu] * 16, axis=0), 0.0)
    cu_turned = cu_square.T
    encode16, decode16, decode64 = cu_square[:16, :16], cu_turned[:16, :16], cu_turned[:64, :64]

    def fold(even, odd):
        total = None
        for value, matrix in ((even, gather[0]), (odd, gather[1])):
            for part in halves(value):
                term = dot(part, matrix)
                total = term if total is None else total + term
        return total

    pl.semaphore_wait(barrier, 15)
    for d in (1, 3):
        signal(relay.at[0], h_peer(d))
    for d in (1, 2, 3):
        signal(relay.at[0], x_peer(d))

    for d in (2, 1, 3):
        send(act, a_in.at[own_rows], xs.at[0], xr.at[0], x_peer(d))
    for c in CHUNKS:
        for d in (2, 1, 3):
            columns = pl.ds(pl.multiple_of(((x + d) % 4) * 1024 + STARTS[c], 128), WIDTHS[c])
            send(cot.at[:, columns], c_in.at[own_rows, pl.ds(STARTS[c], WIDTHS[c])], xs.at[1 + c], xr.at[1 + c], x_peer(d))

    left_high = left.astype(bf16)
    left_mid, left_low = halves(left - left_high.astype(f32))
    local[1].wait()
    own_t = a_own[...].astype(f32).T.astype(bf16)
    mixed_act = jnp.concatenate(halves(dot(left_high, own_t) + dot(left_mid, own_t) + dot(left_low, own_t)), axis=1)
    for at in (2, 3, 4):
        local[at].wait()

    @pl.loop(1, 9)
    def _(d):
        j = (yc + d) % 8
        columns = pl.ds(pl.multiple_of(j * 512, 512), 512)
        mix = dot(mixed_act, c_own[:, columns])
        mix = (mix.reshape(32, 8, 512) * cv512[None]).reshape(256, 512)
        u1[j] = fold(mix[:128], mix[128:])
        rows = exact(encode16, m_in[:, columns]) * decay_rate
        own = fold(rows[:8] * cv512, rows[8:] * cv512)
        at = pl.ds(pl.multiple_of(f * 8, 8), 8)
        u1[j, at, :] = u1[j, at, :] + own

        @pl.when(d < 8)
        def _():
            send(u1.at[j], u1r.at[yc], u1_s, u1_r, yc_peer(d))

    pl.semaphore_wait(relay.at[0], 5)
    for d in (1, 2, 3):
        signal(relay.at[1], x_peer(d))

    local[5].wait()
    wait_bytes(a_in.at[0:384], xr.at[0])
    act_t = a_in[...].astype(f32).T.astype(bf16)
    local[6].wait()

    def products(c):
        width, groups = WIDTHS[c], WIDTHS[c] // 128
        wait_bytes(c_in.at[0:384, pl.ds(STARTS[c], width)], xr.at[1 + c])
        grad = dot(act_t, c_in[:, STARTS[c]:STARTS[c] + width]).reshape(16, 16, width)
        size = jnp.abs(grad)
        size = functools.reduce(jnp.maximum, [size[:, :, 128 * g:128 * (g + 1)] for g in range(groups)])
        size = jnp.maximum(jnp.max(size, axis=1, keepdims=True), 1e-33)
        sc[c] = size * (1.0 / 32767.0)
        inverse = jnp.concatenate([32767.0 / size] * groups, axis=2)
        q[c][...] = jnp.round(grad * inverse).astype(jnp.int32).astype(jnp.int16)
        qr[c][pl.ds(f, 1)] = q[c][pl.ds(f, 1)]
        scr[c, pl.ds(f, 1)] = sc[c, pl.ds(f, 1)]

    def send_products(c):
        @pl.loop(1, 16)
        def _(d):
            who = fsdp_peer(d)
            send(sc.at[c, who[1]], scr.at[c, f], sc_s.at[c], sc_r.at[c], who)
            send(q[c].at[who[1]], qr[c].at[f], q_s.at[c], q_r.at[c], who)

    products(0)
    pl.semaphore_wait(relay.at[1], 3)
    send_products(0)

    u1r[pl.ds(yc, 1)] = u1[pl.ds(yc, 1)]
    wait_bytes(u1r.at[0:7], u1_r)
    u2[...] = functools.reduce(jnp.add, [u1r[i] for i in range(8)]).reshape(16, 8, 128)

    @pl.loop(1, 16)
    def _(d):
        who = fsdp_peer(d)
        send(u2.at[who[1]], u2r.at[f], u2_s, u2_r, who)

    u2r[pl.ds(f, 1)] = u2[pl.ds(f, 1)]

    products(1)
    send_products(1)

    wait_bytes(u2r.at[0:15], u2_r)
    s3[pl.ds(zl, 1)] = functools.reduce(jnp.add, [u2r[i] for i in range(16)])[None]
    for d in (2, 1, 3):
        send(s3.at[zl], s3.at[zl], s3_s, s3_r, z_peer(d))
    wait_bytes(s3.at[0:3], s3_r)
    s4[pl.ds(yc, 1)] = functools.reduce(jnp.add, [s3[i] for i in range(4)])[None]

    @pl.loop(1, 8)
    def _(d):
        send(s4.at[yc], s4.at[yc], s4_s, s4_r, yc_peer(d))

    def new_momentum(c):
        width, groups = WIDTHS[c], WIDTHS[c] // 128
        wait_bytes(scr.at[c, 0:15], sc_r.at[c])
        wait_bytes(qr[c].at[0:15], q_r.at[c])
        strips = []
        for xx in range(4):
            start = 1024 * xx + STARTS[c]
            accrued = decay_rate * m_in[:, start:start + width]
            for hh in range(4):
                scale = jnp.concatenate([scr[c, 4 * hh + xx]] * groups, axis=1)
                accrued = accrued + qr[c][4 * hh + xx].astype(jnp.int32).astype(f32) * scale
            strips.append(accrued)
        accrued = jnp.concatenate(strips, axis=1)
        weight = jnp.concatenate([jnp.concatenate([cv] * 2, axis=0)] * (4 * groups), axis=1)
        rows = exact(encode16, accrued) * weight
        tall = jnp.concatenate([rows[:, 128 * g:128 * (g + 1)] for g in range(4 * groups)], axis=0)
        tall = functools.reduce(jnp.add, [dot(part, block_sum) for part in halves(tall)])
        rows = jnp.concatenate([tall[16 * g:16 * (g + 1)] for g in range(4 * groups)], axis=1)
        left_over = accrued - exact(decode16, rows * weight)
        for xx in range(4):
            start = 1024 * xx + STARTS[c]
            mo_v[:, start:start + width] = left_over[:, xx * width:(xx + 1) * width]

    new_momentum(0)

    wait_bytes(s4.at[0:7], s4_r)
    total = s4[...]
    power = jnp.sum(total * total, axis=1, keepdims=True)
    scaled = halves((total / jnp.sqrt(power * (1.0 / 64.0) + 1e-06)).reshape(64, 128))
    for p in range(2):
        spread = ((iota((128, 512), 1) >> 3) + 64 * p == iota((128, 512), 0)).astype(bf16)
        wide = dot(scaled[0], spread) + dot(scaled[1], spread)
        wide = (wide.reshape(8, 8, 512) * cv512[None]).reshape(64, 512)
        wide = jnp.tanh(exact(decode64, wide))
        for j in range(8):
            mo_half = wide[8 * j:8 * j + 8]
            upd_v[8 * p:8 * p + 8, 512 * j:512 * (j + 1)] = mo_half.astype(bf16)
    out0 = pltpu.make_async_copy(upd_v, upd, out_sem.at[0])
    out0.start()

    new_momentum(1)
    out1 = pltpu.make_async_copy(mo_v, mo, out_sem.at[1])
    out1.start()

    wait_bytes(a_in.at[0:384], xs.at[0])
    for c in CHUNKS:
        wait_bytes(c_in.at[0:384, pl.ds(STARTS[c], WIDTHS[c])], xs.at[1 + c])
        wait_bytes(sc.at[c, 0:15], sc_s.at[c])
        wait_bytes(q[c].at[0:15], q_s.at[c])
    wait_bytes(u1.at[0:7], u1_s)
    wait_bytes(u2.at[0:15], u2_s)
    wait_bytes(s3.at[0:3], s3_s)
    wait_bytes(s4.at[0:7], s4_s)
    out0.wait()
    out1.wait()


def on_device(activations, cotangent, momentum, kept_index):
    hbm = pl.BlockSpec(memory_space=pl.ANY)
    dma = pltpu.SemaphoreType.DMA
    vmem = pltpu.VMEM
    n = len(WIDTHS)
    update, momentum_out = pl.pallas_call(
        kernel,
        name="outer_step",
        out_shape=(jax.ShapeDtypeStruct((16, 4096), bf16), jax.ShapeDtypeStruct((16, 4096), f32)),
        in_specs=[hbm] * 4,
        out_specs=(hbm, hbm),
        scratch_shapes=[
            pltpu.SMEM((8,), jnp.int32),
            vmem((128, 256), bf16),
            vmem((256, 4096), bf16),
            vmem((16, 4096), f32),
            vmem((512, 256), bf16),
            vmem((512, 1024), bf16),
            vmem((8, 128, 128), f32),
            vmem((8, 128, 128), f32),
            vmem((16, 8, 128), f32),
            vmem((16, 8, 128), f32),
            vmem((4, 8, 128), f32),
            vmem((8, 8, 128), f32),
            *[vmem((16, 16, w), jnp.int16) for w in WIDTHS],
            *[vmem((16, 16, w), jnp.int16) for w in WIDTHS],
            vmem((n, 16, 1, 128), f32),
            vmem((n, 16, 1, 128), f32),
            vmem((16, 4096), bf16),
            vmem((16, 4096), f32),
            dma((7,)),
            dma((2,)),
            dma((1 + n,)),
            dma((1 + n,)),
            *[dma] * 8,
            dma((n,)),
            dma((n,)),
            dma((n,)),
            dma((n,)),
            pltpu.SemaphoreType.REGULAR((2,)),
        ],
        compiler_params=pltpu.CompilerParams(
            collective_id=1, has_side_effects=True, vmem_limit_bytes=60 * 1024 * 1024
        ),
    )(kept_index, activations[0], cotangent[0], momentum[0])
    return update, momentum_out[None]


def solution(mesh):
    return jax.shard_map(
        on_device,
        mesh=mesh,
        in_specs=(
            P("replica", "fsdp", None),
            P("replica", "fsdp", None),
            P("replica", "fsdp", None),
            P(),
        ),
        out_specs=(P("fsdp", None), P("replica", "fsdp", None)),
        check_vma=False,
    )
```

```python
import functools
import math

import jax
import jax.numpy as jnp
from jax import lax
from jax.experimental import pallas as pl
from jax.experimental.pallas import tpu as pltpu
from jax.sharding import PartitionSpec as P

MESH = pl.DeviceIdType.MESH
decay_rate = 0.999
f32, bf16 = jnp.float32, jnp.bfloat16
WIDTHS = (256, 256, 256, 256)
STARTS = tuple(sum(WIDTHS[:c]) for c in range(len(WIDTHS)))
CHUNKS = range(len(WIDTHS))


def halves(value):
    high = value.astype(bf16)
    return high, (value - high.astype(f32)).astype(bf16)


def dot(a, b):
    return jnp.dot(a, b, preferred_element_type=f32)


def mix_rows(columns, value):
    wide = [jnp.concatenate([c] * (value.shape[-1] // 128), axis=1) for c in columns]
    return functools.reduce(jnp.add, [w * value[..., i:i + 1, :] for i, w in enumerate(wide)])


def iota(shape, dim):
    return lax.broadcasted_iota(jnp.int32, shape, dim)


def wait_bytes(ref, sem):
    pltpu.make_async_copy(ref, ref, sem).wait()


def cosine_table():
    u = iota((8, 128), 0)
    angle = ((2 * (iota((8, 128), 1) & 7) + 1) * u) & 31
    value = jnp.zeros((8, 128), f32)
    for m in range(32):
        value = jnp.where(angle == m, math.cos(math.pi * m / 16), value)
    return jnp.where(u == 0, math.sqrt(1.0 / 8.0), 0.5 * value)


def kernel(kept_hbm, act, cot, mom, upd, mo, kept, a_own, c_own, m_in, a_in, c_in, u1, u1r, u2, u2r, s3, s4,
           g, q, qr, qh, sc, scr, sch, upd_v, mo_v, local_sem, out_sem, xs, xr, u1_s, u1_r, u2_s, u2_r, s3_s, s3_r,
           s4_s, s4_r, q_s, q_r, qh_s, qh_r, sc_s, sc_r, sch_s, sch_r, relay):
    r, f = lax.axis_index("replica"), lax.axis_index("fsdp")
    zl, yc, h, x = r // 8, r % 8, f // 4, f % 4
    own_rows = pl.ds(pl.multiple_of(x * 128, 128), 128)
    local = [
        pltpu.make_async_copy(kept_hbm, kept, local_sem.at[0]),
        pltpu.make_async_copy(act, a_own, local_sem.at[1]),
        pltpu.make_async_copy(cot, c_own.at[0:128], local_sem.at[2]),
        pltpu.make_async_copy(cot, c_own.at[128:256], local_sem.at[3]),
        pltpu.make_async_copy(mom, m_in, local_sem.at[4]),
        pltpu.make_async_copy(act, a_in.at[own_rows], local_sem.at[5]),
        pltpu.make_async_copy(cot.at[:, pl.ds(pl.multiple_of(x * 1024, 1024), 1024)], c_in.at[own_rows], local_sem.at[6]),
    ]

    def signal(sem, who):
        pl.semaphore_signal(sem, inc=1, device_id=who, device_id_type=MESH)

    def send(src, dst, ssem, rsem, who):
        pltpu.make_async_remote_copy(
            src_ref=src, dst_ref=dst, send_sem=ssem, recv_sem=rsem, device_id=who, device_id_type=MESH
        ).start()

    def fsdp_peer(d):
        return (r, (f + d) % 16)

    def x_peer(d):
        return (r, h * 4 + (x + d) % 4)

    def h_peer(d):
        return (r, ((h + d) % 4) * 4 + x)

    def yc_peer(d):
        return (zl * 8 + (yc + d) % 8, f)

    def z_peer(d):
        return (((zl + d) % 4) * 8 + yc, f)

    barrier = pltpu.get_barrier_semaphore()
    for d in (1, 3):
        signal(barrier, h_peer(d))
    for d in (2, 1, 3):
        signal(barrier, z_peer(d))
        signal(barrier, x_peer(d))

    @pl.loop(1, 8)
    def _(d):
        signal(barrier, yc_peer(d))

    for copy in local:
        copy.start()

    table = cosine_table()
    local[0].wait()
    k_at = iota((8, 128), 0)
    number = jnp.zeros((8, 128), jnp.int32)
    for k in range(8):
        number = jnp.where(k_at == k, kept[k], number)
    row_freq, col_freq = number >> 3, number & 7
    cu = jnp.zeros((8, 128), f32)
    cv = jnp.zeros((8, 128), f32)
    for u in range(8):
        line = jnp.broadcast_to(table[u:u + 1, :], (8, 128))
        cu = jnp.where(row_freq == u, line, cu)
        cv = jnp.where(col_freq == u, line, cv)
    cv512 = jnp.concatenate([cv] * 4, axis=1)
    row_at = iota((256, 256), 0)
    row_block = ((row_at >> 3) & 15) * 2 + (row_at >> 7)
    cu_tall = jnp.concatenate([jnp.concatenate([cu] * 2, axis=1)] * 32, axis=0)
    left = jnp.where((iota((256, 256), 1) >> 3) == row_block, cu_tall, 0.0)
    gather = ((iota((512, 128), 0) >> 3) == iota((512, 128), 1)).astype(bf16)
    block_sum = ((iota((128, 128), 0) >> 3) == (iota((128, 128), 1) >> 3)).astype(bf16)
    encode_rows = [jnp.broadcast_to(cu[:, i:i + 1], (8, 128)) for i in range(8)]
    cu_turned = jnp.concatenate([cu] * 16, axis=0).T[:8, :8]
    decode_rows = [jnp.broadcast_to(cu_turned[:, k:k + 1], (8, 128)) for k in range(8)]

    def two_part(value, matrix):
        n = value.shape[0]
        both = dot(jnp.concatenate(halves(value), axis=0), matrix)
        return both[:n] + both[n:]

    pl.semaphore_wait(barrier, 15)
    for d in (1, 3):
        signal(relay.at[0], h_peer(d))
    for d in (1, 2, 3):
        signal(relay.at[0], x_peer(d))

    for d in (2, 1, 3):
        send(act, a_in.at[own_rows], xs.at[0], xr.at[0], x_peer(d))
    for c in CHUNKS:
        for d in (2, 1, 3):
            columns = pl.ds(pl.multiple_of(((x + d) % 4) * 1024 + STARTS[c], 128), WIDTHS[c])
            send(cot.at[:, columns], c_in.at[own_rows, pl.ds(STARTS[c], WIDTHS[c])], xs.at[1 + c], xr.at[1 + c], x_peer(d))

    left_high = left.astype(bf16)
    left_mid, left_low = halves(left - left_high.astype(f32))
    local[1].wait()
    own_t = a_own[...].astype(f32).T.astype(bf16)
    mixed_act = jnp.concatenate(halves(dot(left_high, own_t) + dot(left_mid, own_t) + dot(left_low, own_t)), axis=1)
    for at in (2, 3, 4):
        local[at].wait()

    @pl.loop(1, 9)
    def _(d):
        j = (yc + d) % 8
        columns = pl.ds(pl.multiple_of(j * 512, 512), 512)
        mix = dot(mixed_act, c_own[:, columns])
        rows = mix_rows(encode_rows, (m_in[:, columns] * decay_rate).reshape(2, 8, 512))
        mix = (jnp.concatenate([mix.reshape(32, 8, 512), rows], axis=0) * cv512[None]).reshape(272, 512)
        sums = two_part(mix, gather)
        u1[j] = sums[:128] + pltpu.roll(sums[128:256], 64, 1)
        at = pl.ds(pl.multiple_of(f * 8, 8), 8)
        u1[j, at, :] = u1[j, at, :] + sums[256:264] + pltpu.roll(sums[264:272], 64, 1)

        @pl.when(d < 8)
        def _():
            send(u1.at[j], u1r.at[yc], u1_s, u1_r, yc_peer(d))

    pl.semaphore_wait(relay.at[0], 5)
    for d in (1, 2, 3):
        signal(relay.at[1], x_peer(d))

    local[5].wait()
    wait_bytes(a_in.at[0:384], xr.at[0])
    act_t = a_in[...].astype(f32).T.astype(bf16)
    local[6].wait()

    up, down, across = (h + 1) % 4, (h + 3) % 4, (h + 2) % 4

    def quantize(c, at, grad):
        groups = WIDTHS[c] // 128
        size = jnp.abs(grad)
        size = functools.reduce(jnp.maximum, [size[:, :, 128 * i:128 * (i + 1)] for i in range(groups)])
        size = jnp.maximum(jnp.max(size, axis=1, keepdims=True), 1e-33)
        sc[c, at] = size * (1.0 / 32767.0)
        inverse = jnp.concatenate([32767.0 / size] * groups, axis=2)
        q[c][at] = jnp.round(grad * inverse).astype(jnp.int32).astype(jnp.int16)

    def restore(c, value, scale):
        return value.astype(jnp.int32).astype(f32) * jnp.concatenate([scale] * (WIDTHS[c] // 128), axis=-1)

    def send_block(c, hh, xx, slot):
        at, who = hh * 4 + xx, (r, hh * 4 + xx)
        send(sc.at[c, at], scr.at[c, slot], sc_s.at[c], sc_r.at[c], who)
        send(q[c].at[at], qr[c].at[slot], q_s.at[c], q_r.at[c], who)

    def products(c):
        wait_bytes(c_in.at[0:384, pl.ds(STARTS[c], WIDTHS[c])], xr.at[1 + c])
        grad = dot(act_t, c_in[:, STARTS[c]:STARTS[c] + WIDTHS[c]]).reshape(16, 16, WIDTHS[c])
        g[c][...] = grad
        quantize(c, slice(None), grad)
        for side, hh in ((0, up), (1, down)):
            at, who = pl.ds(across * 4 + 2 * side, 2), (r, hh * 4 + x)
            send(sc.at[c, at], sch.at[c, side], sch_s.at[c, side], sch_r.at[c, side], who)
            send(q[c].at[at], qh[c].at[side], qh_s.at[c, side], qh_r.at[c, side], who)

    def send_plain(c):
        for xx in (2, 3):
            send_block(c, up, xx, x)
            send_block(c, down, xx - 2, 4 + x)
        for d in (2, 1, 3):
            send_block(c, h, (x + d) % 4, 8 + x)
        qr[c][pl.ds(8 + x, 1)] = q[c][pl.ds(f, 1)]
        scr[c, pl.ds(8 + x, 1)] = sc[c, pl.ds(f, 1)]

    def send_sums(c):
        for side, hh in ((0, up), (1, down)):
            at = pl.ds(hh * 4 + 2 * side, 2)
            wait_bytes(sch.at[c, side], sch_r.at[c, side])
            wait_bytes(qh[c].at[side], qh_r.at[c, side])
            quantize(c, at, g[c][at] + restore(c, qh[c][side], sch[c, side]))
            for xx in (0, 1):
                send_block(c, hh, xx + 2 * side, 4 * side + x)

    products(0)
    pl.semaphore_wait(relay.at[1], 3)
    send_plain(0)

    u1r[pl.ds(yc, 1)] = u1[pl.ds(yc, 1)]
    wait_bytes(u1r.at[0:7], u1_r)
    u2[...] = functools.reduce(jnp.add, [u1r[i] for i in range(8)]).reshape(16, 8, 128)

    @pl.loop(1, 16)
    def _(d):
        who = fsdp_peer(d)
        send(u2.at[who[1]], u2r.at[f], u2_s, u2_r, who)

    u2r[pl.ds(f, 1)] = u2[pl.ds(f, 1)]

    products(1)
    send_plain(1)
    products(2)
    send_plain(2)
    send_sums(0)
    products(3)
    send_plain(3)
    send_sums(1)
    send_sums(2)

    wait_bytes(u2r.at[0:15], u2_r)
    s3[pl.ds(zl, 1)] = functools.reduce(jnp.add, [u2r[i] for i in range(16)])[None]
    for d in (2, 1, 3):
        send(s3.at[zl], s3.at[zl], s3_s, s3_r, z_peer(d))
    send_sums(3)
    wait_bytes(s3.at[0:3], s3_r)
    s4[pl.ds(yc, 1)] = functools.reduce(jnp.add, [s3[i] for i in range(4)])[None]

    @pl.loop(1, 8)
    def _(d):
        send(s4.at[yc], s4.at[yc], s4_s, s4_r, yc_peer(d))

    def new_momentum(c):
        width, groups = WIDTHS[c], WIDTHS[c] // 128
        wait_bytes(scr.at[c, 0:11], sc_r.at[c])
        wait_bytes(qr[c].at[0:11], q_r.at[c])
        strips = []
        for xx in range(4):
            start = 1024 * xx + STARTS[c]
            accrued = decay_rate * m_in[:, start:start + width]
            for slot in (xx, 4 + xx, 8 + xx):
                accrued = accrued + restore(c, qr[c][slot], scr[c, slot])
            strips.append(accrued)
        accrued = jnp.concatenate(strips, axis=1)
        weight = jnp.concatenate([cv] * (4 * groups), axis=1)[None]
        rows = (mix_rows(encode_rows, accrued.reshape(2, 8, 4 * width)) * weight).reshape(16, 4 * width)
        tall = jnp.concatenate([rows[:, 128 * g:128 * (g + 1)] for g in range(4 * groups)], axis=0)
        tall = two_part(tall, block_sum)
        rows = jnp.concatenate([tall[16 * g:16 * (g + 1)] for g in range(4 * groups)], axis=1)
        rows = rows.reshape(2, 8, 4 * width) * weight
        left_over = accrued - mix_rows(decode_rows, rows).reshape(16, 4 * width)
        for xx in range(4):
            start = 1024 * xx + STARTS[c]
            mo_v[:, start:start + width] = left_over[:, xx * width:(xx + 1) * width]

    for c in CHUNKS[:-1]:
        new_momentum(c)

    wait_bytes(s4.at[0:7], s4_r)
    total = s4[...]
    power = jnp.sum(total * total, axis=1, keepdims=True)
    scaled = (total / jnp.sqrt(power * (1.0 / 64.0) + 1e-06)).reshape(64, 128)
    bands = []
    for p in range(2):
        spread = ((iota((128, 512), 1) >> 3) + 64 * p == iota((128, 512), 0)).astype(bf16)
        wide = two_part(scaled, spread).reshape(8, 8, 512) * cv512[None]
        bands.append(jnp.tanh(mix_rows(decode_rows, wide)))
    for j in range(8):
        upd_v[:, 512 * j:512 * (j + 1)] = jnp.concatenate([band[j] for band in bands], axis=0).astype(bf16)
    out0 = pltpu.make_async_copy(upd_v, upd, out_sem.at[0])
    out0.start()

    new_momentum(CHUNKS[-1])
    out1 = pltpu.make_async_copy(mo_v, mo, out_sem.at[1])
    out1.start()

    wait_bytes(a_in.at[0:384], xs.at[0])
    for c in CHUNKS:
        wait_bytes(c_in.at[0:384, pl.ds(STARTS[c], WIDTHS[c])], xs.at[1 + c])
        wait_bytes(sc.at[c, 0:11], sc_s.at[c])
        wait_bytes(q[c].at[0:11], q_s.at[c])
        for side in range(2):
            wait_bytes(sch.at[c, side], sch_s.at[c, side])
            wait_bytes(qh[c].at[side], qh_s.at[c, side])
    wait_bytes(u1.at[0:7], u1_s)
    wait_bytes(u2.at[0:15], u2_s)
    wait_bytes(s3.at[0:3], s3_s)
    wait_bytes(s4.at[0:7], s4_s)
    out0.wait()
    out1.wait()


def on_device(activations, cotangent, momentum, kept_index):
    hbm = pl.BlockSpec(memory_space=pl.ANY)
    dma = pltpu.SemaphoreType.DMA
    vmem = pltpu.VMEM
    n = len(WIDTHS)
    update, momentum_out = pl.pallas_call(
        kernel,
        name="outer_step",
        out_shape=(jax.ShapeDtypeStruct((16, 4096), bf16), jax.ShapeDtypeStruct((16, 4096), f32)),
        in_specs=[hbm] * 4,
        out_specs=(hbm, hbm),
        scratch_shapes=[
            pltpu.SMEM((8,), jnp.int32),
            vmem((128, 256), bf16),
            vmem((256, 4096), bf16),
            vmem((16, 4096), f32),
            vmem((512, 256), bf16),
            vmem((512, 1024), bf16),
            vmem((8, 128, 128), f32),
            vmem((8, 128, 128), f32),
            vmem((16, 8, 128), f32),
            vmem((16, 8, 128), f32),
            vmem((4, 8, 128), f32),
            vmem((8, 8, 128), f32),
            [vmem((16, 16, w), f32) for w in WIDTHS],
            [vmem((16, 16, w), jnp.int16) for w in WIDTHS],
            [vmem((12, 16, w), jnp.int16) for w in WIDTHS],
            [vmem((2, 2, 16, w), jnp.int16) for w in WIDTHS],
            vmem((n, 16, 1, 128), f32),
            vmem((n, 12, 1, 128), f32),
            vmem((n, 2, 2, 1, 128), f32),
            vmem((16, 4096), bf16),
            vmem((16, 4096), f32),
            dma((7,)),
            dma((2,)),
            dma((1 + n,)),
            dma((1 + n,)),
            *[dma] * 8,
            dma((n,)),
            dma((n,)),
            dma((n, 2)),
            dma((n, 2)),
            dma((n,)),
            dma((n,)),
            dma((n, 2)),
            dma((n, 2)),
            pltpu.SemaphoreType.REGULAR((2,)),
        ],
        compiler_params=pltpu.CompilerParams(
            collective_id=1, has_side_effects=True, vmem_limit_bytes=60 * 1024 * 1024
        ),
    )(kept_index, activations[0], cotangent[0], momentum[0])
    return update, momentum_out[None]


def solution(mesh):
    return jax.shard_map(
        on_device,
        mesh=mesh,
        in_specs=(
            P("replica", "fsdp", None),
            P("replica", "fsdp", None),
            P("replica", "fsdp", None),
            P(),
        ),
        out_specs=(P("fsdp", None), P("replica", "fsdp", None)),
        check_vma=False,
    )
```

```python
import functools
import math

import jax
import jax.numpy as jnp
from jax import lax
from jax.experimental import pallas as pl
from jax.experimental.pallas import tpu as pltpu
from jax.sharding import PartitionSpec as P

MESH = pl.DeviceIdType.MESH
decay_rate = 0.999
f32, bf16 = jnp.float32, jnp.bfloat16
WIDTHS = (256, 384, 384)
STARTS = tuple(sum(WIDTHS[:c]) for c in range(len(WIDTHS)))
CHUNKS = range(len(WIDTHS))
ORDER = "P0 U2 P1 A0 P2 S3 A1 S4 A2 X M0 M1 UP M2"


def halves(value):
    high = value.astype(bf16)
    return high, (value - high.astype(f32)).astype(bf16)


def dot(a, b):
    return jnp.dot(a, b, preferred_element_type=f32)


def mix_rows(columns, value):
    wide = [jnp.concatenate([c] * (value.shape[-1] // 128), axis=1) for c in columns]
    return functools.reduce(jnp.add, [w * value[..., i:i + 1, :] for i, w in enumerate(wide)])


def iota(shape, dim):
    return lax.broadcasted_iota(jnp.int32, shape, dim)


def wait_bytes(ref, sem):
    pltpu.make_async_copy(ref, ref, sem).wait()


def cosine_table():
    u = iota((8, 128), 0)
    angle = ((2 * (iota((8, 128), 1) & 7) + 1) * u) & 31
    value = jnp.zeros((8, 128), f32)
    for m in range(32):
        value = jnp.where(angle == m, math.cos(math.pi * m / 16), value)
    return jnp.where(u == 0, math.sqrt(1.0 / 8.0), 0.5 * value)


def kernel(kept_hbm, act, cot, mom, upd, mo, kept, a_own, c_own, m_in, a_in, c_in, u1, u1r, u2, u2r, s3, s4,
           g, q, qr, qh, sc, scr, sch, upd_v, mo_v, local_sem, out_sem, xs, xr, u1_s, u1_r, u2_s, u2_r, s3_s, s3_r,
           s4_s, s4_r, q_s, q_r, qh_s, qh_r, sc_s, sc_r, sch_s, sch_r, relay):
    r, f = lax.axis_index("replica"), lax.axis_index("fsdp")
    zl, yc, h, x = r // 8, r % 8, f // 4, f % 4
    own_rows = pl.ds(pl.multiple_of(x * 128, 128), 128)
    local = [
        pltpu.make_async_copy(kept_hbm, kept, local_sem.at[0]),
        pltpu.make_async_copy(act, a_own, local_sem.at[1]),
        pltpu.make_async_copy(cot, c_own.at[0:128], local_sem.at[2]),
        pltpu.make_async_copy(cot, c_own.at[128:256], local_sem.at[3]),
        pltpu.make_async_copy(mom, m_in, local_sem.at[4]),
        pltpu.make_async_copy(act, a_in.at[own_rows], local_sem.at[5]),
        pltpu.make_async_copy(cot.at[:, pl.ds(pl.multiple_of(x * 1024, 1024), 1024)], c_in.at[own_rows], local_sem.at[6]),
    ]

    def signal(sem, who):
        pl.semaphore_signal(sem, inc=1, device_id=who, device_id_type=MESH)

    def send(src, dst, ssem, rsem, who):
        pltpu.make_async_remote_copy(
            src_ref=src, dst_ref=dst, send_sem=ssem, recv_sem=rsem, device_id=who, device_id_type=MESH
        ).start()

    def fsdp_peer(d):
        return (r, (f + d) % 16)

    def x_peer(d):
        return (r, h * 4 + (x + d) % 4)

    def h_peer(d):
        return (r, ((h + d) % 4) * 4 + x)

    def yc_peer(d):
        return (zl * 8 + (yc + d) % 8, f)

    def z_peer(d):
        return (((zl + d) % 4) * 8 + yc, f)

    barrier = pltpu.get_barrier_semaphore()
    for d in (1, 3):
        signal(barrier, h_peer(d))
    for d in (2, 1, 3):
        signal(barrier, z_peer(d))
        signal(barrier, x_peer(d))

    @pl.loop(1, 8)
    def _(d):
        signal(barrier, yc_peer(d))

    for copy in local:
        copy.start()

    table = cosine_table()
    local[0].wait()
    k_at = iota((8, 128), 0)
    number = jnp.zeros((8, 128), jnp.int32)
    for k in range(8):
        number = jnp.where(k_at == k, kept[k], number)
    row_freq, col_freq = number >> 3, number & 7
    cu = jnp.zeros((8, 128), f32)
    cv = jnp.zeros((8, 128), f32)
    for u in range(8):
        line = jnp.broadcast_to(table[u:u + 1, :], (8, 128))
        cu = jnp.where(row_freq == u, line, cu)
        cv = jnp.where(col_freq == u, line, cv)
    cv512 = jnp.concatenate([cv] * 4, axis=1)
    row_at = iota((256, 256), 0)
    row_block = ((row_at >> 3) & 15) * 2 + (row_at >> 7)
    cu_tall = jnp.concatenate([jnp.concatenate([cu] * 2, axis=1)] * 32, axis=0)
    left = jnp.where((iota((256, 256), 1) >> 3) == row_block, cu_tall, 0.0)
    gather = ((iota((512, 128), 0) >> 3) == iota((512, 128), 1)).astype(bf16)
    block_sum = ((iota((128, 128), 0) >> 3) == (iota((128, 128), 1) >> 3)).astype(bf16)
    encode_rows = [jnp.broadcast_to(cu[:, i:i + 1], (8, 128)) for i in range(8)]
    cu_turned = jnp.concatenate([cu] * 16, axis=0).T[:8, :8]
    decode_rows = [jnp.broadcast_to(cu_turned[:, k:k + 1], (8, 128)) for k in range(8)]

    def two_part(value, matrix):
        n = value.shape[0]
        both = dot(jnp.concatenate(halves(value), axis=0), matrix)
        return both[:n] + both[n:]

    pl.semaphore_wait(barrier, 15)
    for d in (1, 3):
        signal(relay.at[0], h_peer(d))
    for d in (1, 2, 3):
        signal(relay.at[0], x_peer(d))

    for d in (2, 1, 3):
        send(act, a_in.at[own_rows], xs.at[0], xr.at[0], x_peer(d))
    for c in CHUNKS:
        for d in (2, 1, 3):
            columns = pl.ds(pl.multiple_of(((x + d) % 4) * 1024 + STARTS[c], 128), WIDTHS[c])
            send(cot.at[:, columns], c_in.at[own_rows, pl.ds(STARTS[c], WIDTHS[c])], xs.at[1 + c], xr.at[1 + c], x_peer(d))

    left_high = left.astype(bf16)
    left_mid, left_low = halves(left - left_high.astype(f32))
    local[1].wait()
    own_t = a_own[...].astype(f32).T.astype(bf16)
    mixed_act = jnp.concatenate(halves(dot(left_high, own_t) + dot(left_mid, own_t) + dot(left_low, own_t)), axis=1)
    for at in (2, 3, 4):
        local[at].wait()

    @pl.loop(1, 9)
    def _(d):
        j = (yc + d) % 8
        columns = pl.ds(pl.multiple_of(j * 512, 512), 512)
        mix = dot(mixed_act, c_own[:, columns])
        rows = mix_rows(encode_rows, (m_in[:, columns] * decay_rate).reshape(2, 8, 512))
        mix = (jnp.concatenate([mix.reshape(32, 8, 512), rows], axis=0) * cv512[None]).reshape(272, 512)
        sums = two_part(mix, gather)
        u1[j] = sums[:128] + pltpu.roll(sums[128:256], 64, 1)
        at = pl.ds(pl.multiple_of(f * 8, 8), 8)
        u1[j, at, :] = u1[j, at, :] + sums[256:264] + pltpu.roll(sums[264:272], 64, 1)

        @pl.when(d < 8)
        def _():
            send(u1.at[j], u1r.at[yc], u1_s, u1_r, yc_peer(d))

    local[5].wait()
    wait_bytes(a_in.at[0:384], xr.at[0])
    act_t = a_in[...].astype(f32).T.astype(bf16)
    local[6].wait()

    up, down, across = (h + 1) % 4, (h + 3) % 4, (h + 2) % 4

    def quantize(c, at, grad):
        groups = WIDTHS[c] // 128
        size = jnp.abs(grad)
        size = functools.reduce(jnp.maximum, [size[:, :, 128 * i:128 * (i + 1)] for i in range(groups)])
        size = jnp.maximum(jnp.max(size, axis=1, keepdims=True), 1e-33)
        sc[c, at] = size * (1.0 / 32767.0)
        inverse = jnp.concatenate([32767.0 / size] * groups, axis=2)
        q[c][at] = jnp.round(grad * inverse).astype(jnp.int32).astype(jnp.int16)

    def restore(c, value, scale):
        return value.astype(jnp.int32).astype(f32) * jnp.concatenate([scale] * (WIDTHS[c] // 128), axis=-1)

    def send_block(c, hh, xx, slot):
        at, who = hh * 4 + xx, (r, hh * 4 + xx)
        send(sc.at[c, at], scr.at[c, slot], sc_s.at[c], sc_r.at[c], who)
        send(q[c].at[at], qr[c].at[slot], q_s.at[c], q_r.at[c], who)

    def products(c):
        wait_bytes(c_in.at[0:384, pl.ds(STARTS[c], WIDTHS[c])], xr.at[1 + c])
        grad = dot(act_t, c_in[:, STARTS[c]:STARTS[c] + WIDTHS[c]]).reshape(16, 16, WIDTHS[c])
        g[c][...] = grad
        quantize(c, slice(None), grad)
        for side, hh in ((0, up), (1, down)):
            at, who = pl.ds(across * 4 + 2 * side, 2), (r, hh * 4 + x)
            send(sc.at[c, at], sch.at[c, side], sch_s.at[c, side], sch_r.at[c, side], who)
            send(q[c].at[at], qh[c].at[side], qh_s.at[c, side], qh_r.at[c, side], who)
        if c == 0:
            pl.semaphore_wait(relay.at[0], 5)
            for d in (1, 2, 3):
                signal(relay.at[1], x_peer(d))
        for xx in (2, 3):
            send_block(c, up, xx, x)
            send_block(c, down, xx - 2, 4 + x)
        qr[c][pl.ds(8 + x, 1)] = q[c][pl.ds(f, 1)]
        scr[c, pl.ds(8 + x, 1)] = sc[c, pl.ds(f, 1)]

    def send_beside():
        for c in CHUNKS:
            for d in (2, 1, 3):
                send_block(c, h, (x + d) % 4, 8 + x)

    def send_sums(c):
        for side, hh in ((0, up), (1, down)):
            at = pl.ds(hh * 4 + 2 * side, 2)
            wait_bytes(sch.at[c, side], sch_r.at[c, side])
            wait_bytes(qh[c].at[side], qh_r.at[c, side])
            quantize(c, at, g[c][at] + restore(c, qh[c][side], sch[c, side]))
            for xx in (0, 1):
                send_block(c, hh, xx + 2 * side, 4 * side + x)

    def sum_fsdp():
        pl.semaphore_wait(relay.at[1], 3)
        u1r[pl.ds(yc, 1)] = u1[pl.ds(yc, 1)]
        wait_bytes(u1r.at[0:7], u1_r)
        u2[...] = functools.reduce(jnp.add, [u1r[i] for i in range(8)]).reshape(16, 8, 128)

        @pl.loop(1, 16)
        def _(d):
            who = fsdp_peer(d)
            send(u2.at[who[1]], u2r.at[f], u2_s, u2_r, who)

        u2r[pl.ds(f, 1)] = u2[pl.ds(f, 1)]

    def sum_z():
        wait_bytes(u2r.at[0:15], u2_r)
        s3[pl.ds(zl, 1)] = functools.reduce(jnp.add, [u2r[i] for i in range(16)])[None]
        for d in (2, 1, 3):
            send(s3.at[zl], s3.at[zl], s3_s, s3_r, z_peer(d))
    def gather_yc():
        wait_bytes(s3.at[0:3], s3_r)
        s4[pl.ds(yc, 1)] = functools.reduce(jnp.add, [s3[i] for i in range(4)])[None]

        @pl.loop(1, 8)
        def _(d):
            send(s4.at[yc], s4.at[yc], s4_s, s4_r, yc_peer(d))

    def new_momentum(c):
        width, groups = WIDTHS[c], WIDTHS[c] // 128
        wait_bytes(scr.at[c, 0:11], sc_r.at[c])
        wait_bytes(qr[c].at[0:11], q_r.at[c])
        strips = []
        for xx in range(4):
            start = 1024 * xx + STARTS[c]
            accrued = decay_rate * m_in[:, start:start + width]
            for slot in (xx, 4 + xx, 8 + xx):
                accrued = accrued + restore(c, qr[c][slot], scr[c, slot])
            strips.append(accrued)
        accrued = jnp.concatenate(strips, axis=1)
        weight = jnp.concatenate([cv] * (4 * groups), axis=1)[None]
        rows = (mix_rows(encode_rows, accrued.reshape(2, 8, 4 * width)) * weight).reshape(16, 4 * width)
        tall = jnp.concatenate([rows[:, 128 * g:128 * (g + 1)] for g in range(4 * groups)], axis=0)
        tall = two_part(tall, block_sum)
        rows = jnp.concatenate([tall[16 * g:16 * (g + 1)] for g in range(4 * groups)], axis=1)
        rows = rows.reshape(2, 8, 4 * width) * weight
        left_over = accrued - mix_rows(decode_rows, rows).reshape(16, 4 * width)
        for xx in range(4):
            start = 1024 * xx + STARTS[c]
            mo_v[:, start:start + width] = left_over[:, xx * width:(xx + 1) * width]
            strip = pl.ds(start, width)
            pltpu.make_async_copy(mo_v.at[:, strip], mo.at[:, strip], out_sem.at[1]).start()

    def update():
        wait_bytes(s4.at[0:7], s4_r)
        total = s4[...]
        power = jnp.sum(total * total, axis=1, keepdims=True)
        scaled = (total / jnp.sqrt(power * (1.0 / 64.0) + 1e-06)).reshape(64, 128)
        bands = []
        for p in range(2):
            spread = ((iota((128, 512), 1) >> 3) + 64 * p == iota((128, 512), 0)).astype(bf16)
            wide = two_part(scaled, spread).reshape(8, 8, 512) * cv512[None]
            bands.append(jnp.tanh(mix_rows(decode_rows, wide)))
        for j in range(8):
            upd_v[:, 512 * j:512 * (j + 1)] = jnp.concatenate([band[j] for band in bands], axis=0).astype(bf16)
        pltpu.make_async_copy(upd_v, upd, out_sem.at[0]).start()

    steps = {"U2": sum_fsdp, "S3": sum_z, "S4": gather_yc, "UP": update, "X": send_beside}
    steps |= {f"P{c}": functools.partial(products, c) for c in CHUNKS}
    steps |= {f"A{c}": functools.partial(send_sums, c) for c in CHUNKS}
    steps |= {f"M{c}": functools.partial(new_momentum, c) for c in CHUNKS}
    for step in ORDER.split():
        steps[step]()

    wait_bytes(a_in.at[0:384], xs.at[0])
    for c in CHUNKS:
        wait_bytes(c_in.at[0:384, pl.ds(STARTS[c], WIDTHS[c])], xs.at[1 + c])
        wait_bytes(sc.at[c, 0:11], sc_s.at[c])
        wait_bytes(q[c].at[0:11], q_s.at[c])
        for side in range(2):
            wait_bytes(sch.at[c, side], sch_s.at[c, side])
            wait_bytes(qh[c].at[side], qh_s.at[c, side])
    wait_bytes(u1.at[0:7], u1_s)
    wait_bytes(u2.at[0:15], u2_s)
    wait_bytes(s3.at[0:3], s3_s)
    wait_bytes(s4.at[0:7], s4_s)
    wait_bytes(upd_v, out_sem.at[0])
    wait_bytes(mo_v, out_sem.at[1])


def hand_over(upd, mo, upd_out, mo_out, upd_v, mo_v, sem):
    pairs = ((mo, mo_v, mo_out), (upd, upd_v, upd_out))
    into = [pltpu.make_async_copy(src, held, sem.at[i]) for i, (src, held, _) in enumerate(pairs)]
    out = [pltpu.make_async_copy(held, dst, sem.at[2 + i]) for i, (_, held, dst) in enumerate(pairs)]
    for copy in into:
        copy.start()
    for before, after in zip(into, out):
        before.wait()
        after.start()
    for copy in out:
        copy.wait()


def on_device(activations, cotangent, momentum, kept_index):
    hbm = pl.BlockSpec(memory_space=pl.ANY)
    dma = pltpu.SemaphoreType.DMA
    vmem = pltpu.VMEM
    n = len(WIDTHS)
    out_shape = (jax.ShapeDtypeStruct((16, 4096), bf16), jax.ShapeDtypeStruct((16, 4096), f32))
    update, momentum_out = pl.pallas_call(
        kernel,
        name="outer_step",
        out_shape=out_shape,
        in_specs=[hbm] * 4,
        out_specs=(hbm, hbm),
        scratch_shapes=[
            pltpu.SMEM((8,), jnp.int32),
            vmem((128, 256), bf16),
            vmem((256, 4096), bf16),
            vmem((16, 4096), f32),
            vmem((512, 256), bf16),
            vmem((512, 1024), bf16),
            vmem((8, 128, 128), f32),
            vmem((8, 128, 128), f32),
            vmem((16, 8, 128), f32),
            vmem((16, 8, 128), f32),
            vmem((4, 8, 128), f32),
            vmem((8, 8, 128), f32),
            [vmem((16, 16, w), f32) for w in WIDTHS],
            [vmem((16, 16, w), jnp.int16) for w in WIDTHS],
            [vmem((12, 16, w), jnp.int16) for w in WIDTHS],
            [vmem((2, 2, 16, w), jnp.int16) for w in WIDTHS],
            vmem((n, 16, 1, 128), f32),
            vmem((n, 12, 1, 128), f32),
            vmem((n, 2, 2, 1, 128), f32),
            vmem((16, 4096), bf16),
            vmem((16, 4096), f32),
            dma((7,)),
            dma((2,)),
            dma((1 + n,)),
            dma((1 + n,)),
            *[dma] * 8,
            dma((n,)),
            dma((n,)),
            dma((n, 2)),
            dma((n, 2)),
            dma((n,)),
            dma((n,)),
            dma((n, 2)),
            dma((n, 2)),
            pltpu.SemaphoreType.REGULAR((2,)),
        ],
        compiler_params=pltpu.CompilerParams(
            collective_id=1, has_side_effects=True, vmem_limit_bytes=60 * 1024 * 1024
        ),
    )(kept_index, activations[0], cotangent[0], momentum[0])
    update, momentum_out = pl.pallas_call(
        hand_over,
        name="hand_over",
        out_shape=out_shape,
        in_specs=[hbm] * 2,
        out_specs=(hbm, hbm),
        scratch_shapes=[vmem((16, 4096), bf16), vmem((16, 4096), f32), dma((4,))],
        compiler_params=pltpu.CompilerParams(vmem_limit_bytes=60 * 1024 * 1024),
    )(update, momentum_out)
    return update, momentum_out[None]


def solution(mesh):
    return jax.shard_map(
        on_device,
        mesh=mesh,
        in_specs=(
            P("replica", "fsdp", None),
            P("replica", "fsdp", None),
            P("replica", "fsdp", None),
            P(),
        ),
        out_specs=(P("fsdp", None), P("replica", "fsdp", None)),
        check_vma=False,
    )
```

```python
import functools
import math

import jax
import jax.numpy as jnp
from jax import lax
from jax.experimental import pallas as pl
from jax.experimental.pallas import tpu as pltpu
from jax.sharding import PartitionSpec as P

MESH = pl.DeviceIdType.MESH
decay_rate = 0.999
f32, bf16 = jnp.float32, jnp.bfloat16
WIDTHS = (128, 384, 512)
STARTS = tuple(sum(WIDTHS[:c]) for c in range(len(WIDTHS)))
CHUNKS = range(len(WIDTHS))
ORDER = ('P0', 'U2', 'P1', 'A0', 'P2', 'S3', 'A1', 'S4', 'A2', 'X', 'M0', 'M1', 'UP', 'M2')


def halves(value):
    high = value.astype(bf16)
    return high, (value - high.astype(f32)).astype(bf16)


def dot(a, b):
    return jnp.dot(a, b, preferred_element_type=f32)


def mix_rows(columns, value):
    wide = [jnp.concatenate([c] * (value.shape[-1] // 128), axis=1) for c in columns]
    return functools.reduce(jnp.add, [w * value[..., i:i + 1, :] for i, w in enumerate(wide)])


def iota(shape, dim):
    return lax.broadcasted_iota(jnp.int32, shape, dim)


def wait_bytes(ref, sem):
    pltpu.make_async_copy(ref, ref, sem).wait()


def cosine_table():
    u = iota((8, 128), 0)
    angle = ((2 * (iota((8, 128), 1) & 7) + 1) * u) & 31
    value = jnp.zeros((8, 128), f32)
    for m in range(32):
        value = jnp.where(angle == m, math.cos(math.pi * m / 16), value)
    return jnp.where(u == 0, math.sqrt(1.0 / 8.0), 0.5 * value)


def kernel(kept_hbm, act, cot, mom, upd, mo, kept, a_own, c_own, m_in, a_in, c_in, u1, u1r, u2, u2r, s3, s4,
           g, q, qr, qh, sc, scr, sch, upd_v, mo_v, local_sem, out_sem, xs, xr, u1_s, u1_r, u2_s, u2_r, s3_s, s3_r,
           s4_s, s4_r, q_s, q_r, qh_s, qh_r, sc_s, sc_r, sch_s, sch_r, relay):
    r, f = lax.axis_index("replica"), lax.axis_index("fsdp")
    zl, yc, h, x = r // 8, r % 8, f // 4, f % 4
    own_rows = pl.ds(pl.multiple_of(x * 128, 128), 128)
    local = [
        pltpu.make_async_copy(kept_hbm, kept, local_sem.at[0]),
        pltpu.make_async_copy(act, a_own, local_sem.at[1]),
        pltpu.make_async_copy(cot, c_own.at[0:128], local_sem.at[2]),
        pltpu.make_async_copy(cot, c_own.at[128:256], local_sem.at[3]),
        pltpu.make_async_copy(mom, m_in, local_sem.at[4]),
        pltpu.make_async_copy(act, a_in.at[own_rows], local_sem.at[5]),
        pltpu.make_async_copy(cot.at[:, pl.ds(pl.multiple_of(x * 1024, 1024), 1024)], c_in.at[own_rows], local_sem.at[6]),
    ]

    def signal(sem, who):
        pl.semaphore_signal(sem, inc=1, device_id=who, device_id_type=MESH)

    def send(src, dst, ssem, rsem, who):
        pltpu.make_async_remote_copy(
            src_ref=src, dst_ref=dst, send_sem=ssem, recv_sem=rsem, device_id=who, device_id_type=MESH
        ).start()

    def fsdp_peer(d):
        return (r, (f + d) % 16)

    def x_peer(d):
        return (r, h * 4 + (x + d) % 4)

    def h_peer(d):
        return (r, ((h + d) % 4) * 4 + x)

    def yc_peer(d):
        return (zl * 8 + (yc + d) % 8, f)

    def z_peer(d):
        return (((zl + d) % 4) * 8 + yc, f)

    barrier = pltpu.get_barrier_semaphore()
    for d in (1, 3):
        signal(barrier, h_peer(d))
    for d in (2, 1, 3):
        signal(barrier, z_peer(d))
        signal(barrier, x_peer(d))

    @pl.loop(1, 8)
    def _(d):
        signal(barrier, yc_peer(d))

    for copy in local:
        copy.start()

    table = cosine_table()
    local[0].wait()
    k_at = iota((8, 128), 0)
    number = jnp.zeros((8, 128), jnp.int32)
    for k in range(8):
        number = jnp.where(k_at == k, kept[k], number)
    row_freq, col_freq = number >> 3, number & 7
    cu = jnp.zeros((8, 128), f32)
    cv = jnp.zeros((8, 128), f32)
    for u in range(8):
        line = jnp.broadcast_to(table[u:u + 1, :], (8, 128))
        cu = jnp.where(row_freq == u, line, cu)
        cv = jnp.where(col_freq == u, line, cv)
    cv512 = jnp.concatenate([cv] * 4, axis=1)
    row_at = iota((256, 256), 0)
    row_block = ((row_at >> 3) & 15) * 2 + (row_at >> 7)
    cu_tall = jnp.concatenate([jnp.concatenate([cu] * 2, axis=1)] * 32, axis=0)
    left = jnp.where((iota((256, 256), 1) >> 3) == row_block, cu_tall, 0.0)
    gather = ((iota((512, 128), 0) >> 3) == iota((512, 128), 1)).astype(bf16)
    block_sum = ((iota((128, 128), 0) >> 3) == (iota((128, 128), 1) >> 3)).astype(bf16)
    encode_rows = [jnp.broadcast_to(cu[:, i:i + 1], (8, 128)) for i in range(8)]
    cu_turned = jnp.concatenate([cu] * 16, axis=0).T[:8, :8]
    decode_rows = [jnp.broadcast_to(cu_turned[:, k:k + 1], (8, 128)) for k in range(8)]

    def two_part(value, matrix):
        n = value.shape[0]
        both = dot(jnp.concatenate(halves(value), axis=0), matrix)
        return both[:n] + both[n:]

    pl.semaphore_wait(barrier, 15)
    for d in (1, 3):
        signal(relay.at[0], h_peer(d))
    for d in (1, 2, 3):
        signal(relay.at[0], x_peer(d))

    for d in (2, 1, 3):
        send(act, a_in.at[own_rows], xs.at[0], xr.at[0], x_peer(d))
    for c in CHUNKS:
        for d in (2, 1, 3):
            columns = pl.ds(pl.multiple_of(((x + d) % 4) * 1024 + STARTS[c], 128), WIDTHS[c])
            send(cot.at[:, columns], c_in.at[own_rows, pl.ds(STARTS[c], WIDTHS[c])], xs.at[1 + c], xr.at[1 + c], x_peer(d))

    left_high = left.astype(bf16)
    left_mid, left_low = halves(left - left_high.astype(f32))
    local[1].wait()
    own_t = a_own[...].astype(f32).T.astype(bf16)
    mixed_act = jnp.concatenate(halves(dot(left_high, own_t) + dot(left_mid, own_t) + dot(left_low, own_t)), axis=1)
    for at in (2, 3, 4):
        local[at].wait()

    @pl.loop(1, 9)
    def _(d):
        j = (yc + d) % 8
        columns = pl.ds(pl.multiple_of(j * 512, 512), 512)
        mix = dot(mixed_act, c_own[:, columns])
        rows = mix_rows(encode_rows, (m_in[:, columns] * decay_rate).reshape(2, 8, 512))
        mix = (jnp.concatenate([mix.reshape(32, 8, 512), rows], axis=0) * cv512[None]).reshape(272, 512)
        sums = two_part(mix, gather)
        u1[j] = sums[:128] + pltpu.roll(sums[128:256], 64, 1)
        at = pl.ds(pl.multiple_of(f * 8, 8), 8)
        u1[j, at, :] = u1[j, at, :] + sums[256:264] + pltpu.roll(sums[264:272], 64, 1)

        @pl.when(d < 8)
        def _():
            send(u1.at[j], u1r.at[yc], u1_s, u1_r, yc_peer(d))

    pl.semaphore_wait(relay.at[0], 5)
    for d in (1, 2, 3):
        signal(relay.at[1], x_peer(d))

    local[5].wait()
    wait_bytes(a_in.at[0:384], xr.at[0])
    act_t = a_in[...].astype(f32).T.astype(bf16)
    local[6].wait()

    up, down, across = (h + 1) % 4, (h + 3) % 4, (h + 2) % 4

    def quantize(c, at, grad):
        groups = WIDTHS[c] // 128
        size = jnp.abs(grad)
        size = functools.reduce(jnp.maximum, [size[:, :, 128 * i:128 * (i + 1)] for i in range(groups)])
        size = jnp.maximum(jnp.max(size, axis=1, keepdims=True), 1e-33)
        sc[c, at] = size * (1.0 / 32767.0)
        inverse = jnp.concatenate([32767.0 / size] * groups, axis=2)
        q[c][at] = jnp.round(grad * inverse).astype(jnp.int32).astype(jnp.int16)

    def restore(c, value, scale):
        return value.astype(jnp.int32).astype(f32) * jnp.concatenate([scale] * (WIDTHS[c] // 128), axis=-1)

    def send_block(c, hh, xx, slot):
        at, who = hh * 4 + xx, (r, hh * 4 + xx)
        send(sc.at[c, at], scr.at[c, slot], sc_s.at[c], sc_r.at[c], who)
        send(q[c].at[at], qr[c].at[slot], q_s.at[c], q_r.at[c], who)

    def products(c):
        wait_bytes(c_in.at[0:384, pl.ds(STARTS[c], WIDTHS[c])], xr.at[1 + c])
        grad = dot(act_t, c_in[:, STARTS[c]:STARTS[c] + WIDTHS[c]]).reshape(16, 16, WIDTHS[c])
        g[c][...] = grad
        quantize(c, slice(None), grad)
        for side, hh in ((0, up), (1, down)):
            at, who = pl.ds(across * 4 + 2 * side, 2), (r, hh * 4 + x)
            send(sc.at[c, at], sch.at[c, side], sch_s.at[c, side], sch_r.at[c, side], who)
            send(q[c].at[at], qh[c].at[side], qh_s.at[c, side], qh_r.at[c, side], who)
        for xx in (2, 3):
            send_block(c, up, xx, x)
            send_block(c, down, xx - 2, 4 + x)
        qr[c][pl.ds(8 + x, 1)] = q[c][pl.ds(f, 1)]
        scr[c, pl.ds(8 + x, 1)] = sc[c, pl.ds(f, 1)]

    def send_beside():
        for c in CHUNKS:
            for d in (2, 1, 3):
                send_block(c, h, (x + d) % 4, 8 + x)

    def send_sums(c):
        for side, hh in ((0, up), (1, down)):
            at = pl.ds(hh * 4 + 2 * side, 2)
            wait_bytes(sch.at[c, side], sch_r.at[c, side])
            wait_bytes(qh[c].at[side], qh_r.at[c, side])
            quantize(c, at, g[c][at] + restore(c, qh[c][side], sch[c, side]))
            for xx in (0, 1):
                send_block(c, hh, xx + 2 * side, 4 * side + x)

    def sum_fsdp():
        pl.semaphore_wait(relay.at[1], 3)
        u1r[pl.ds(yc, 1)] = u1[pl.ds(yc, 1)]
        wait_bytes(u1r.at[0:7], u1_r)
        u2[...] = functools.reduce(jnp.add, [u1r[i] for i in range(8)]).reshape(16, 8, 128)

        @pl.loop(1, 16)
        def _(d):
            who = fsdp_peer(d)
            send(u2.at[who[1]], u2r.at[f], u2_s, u2_r, who)

        u2r[pl.ds(f, 1)] = u2[pl.ds(f, 1)]

    def sum_z():
        wait_bytes(u2r.at[0:15], u2_r)
        s3[pl.ds(zl, 1)] = functools.reduce(jnp.add, [u2r[i] for i in range(16)])[None]
        for d in (2, 1, 3):
            send(s3.at[zl], s3.at[zl], s3_s, s3_r, z_peer(d))
    def gather_yc():
        wait_bytes(s3.at[0:3], s3_r)
        s4[pl.ds(yc, 1)] = functools.reduce(jnp.add, [s3[i] for i in range(4)])[None]

        @pl.loop(1, 8)
        def _(d):
            send(s4.at[yc], s4.at[yc], s4_s, s4_r, yc_peer(d))

    def new_momentum(c):
        width, groups = WIDTHS[c], WIDTHS[c] // 128
        wait_bytes(scr.at[c, 0:11], sc_r.at[c])
        wait_bytes(qr[c].at[0:11], q_r.at[c])
        strips = []
        for xx in range(4):
            start = 1024 * xx + STARTS[c]
            accrued = decay_rate * m_in[:, start:start + width]
            for slot in (xx, 4 + xx, 8 + xx):
                accrued = accrued + restore(c, qr[c][slot], scr[c, slot])
            strips.append(accrued)
        accrued = jnp.concatenate(strips, axis=1)
        weight = jnp.concatenate([cv] * (4 * groups), axis=1)[None]
        rows = (mix_rows(encode_rows, accrued.reshape(2, 8, 4 * width)) * weight).reshape(16, 4 * width)
        tall = jnp.concatenate([rows[:, 128 * g:128 * (g + 1)] for g in range(4 * groups)], axis=0)
        tall = two_part(tall, block_sum)
        rows = jnp.concatenate([tall[16 * g:16 * (g + 1)] for g in range(4 * groups)], axis=1)
        rows = rows.reshape(2, 8, 4 * width) * weight
        left_over = accrued - mix_rows(decode_rows, rows).reshape(16, 4 * width)
        for xx in range(4):
            start = 1024 * xx + STARTS[c]
            mo_v[:, start:start + width] = left_over[:, xx * width:(xx + 1) * width]
            strip = pl.ds(start, width)
            pltpu.make_async_copy(mo_v.at[:, strip], mo.at[:, strip], out_sem.at[1]).start()

    def update():
        wait_bytes(s4.at[0:7], s4_r)
        total = s4[...]
        power = jnp.sum(total * total, axis=1, keepdims=True)
        scaled = (total / jnp.sqrt(power * (1.0 / 64.0) + 1e-06)).reshape(64, 128)
        bands = []
        for p in range(2):
            spread = ((iota((128, 512), 1) >> 3) + 64 * p == iota((128, 512), 0)).astype(bf16)
            wide = two_part(scaled, spread).reshape(8, 8, 512) * cv512[None]
            bands.append(jnp.tanh(mix_rows(decode_rows, wide)))
        for j in range(8):
            upd_v[:, 512 * j:512 * (j + 1)] = jnp.concatenate([band[j] for band in bands], axis=0).astype(bf16)
        pltpu.make_async_copy(upd_v, upd, out_sem.at[0]).start()

    steps = {"U2": sum_fsdp, "S3": sum_z, "S4": gather_yc, "UP": update, "X": send_beside}
    steps |= {f"P{c}": functools.partial(products, c) for c in CHUNKS}
    steps |= {f"A{c}": functools.partial(send_sums, c) for c in CHUNKS}
    steps |= {f"M{c}": functools.partial(new_momentum, c) for c in CHUNKS}
    for step in ORDER:
        steps[step]()

    wait_bytes(a_in.at[0:384], xs.at[0])
    for c in CHUNKS:
        wait_bytes(c_in.at[0:384, pl.ds(STARTS[c], WIDTHS[c])], xs.at[1 + c])
        wait_bytes(sc.at[c, 0:11], sc_s.at[c])
        wait_bytes(q[c].at[0:11], q_s.at[c])
        for side in range(2):
            wait_bytes(sch.at[c, side], sch_s.at[c, side])
            wait_bytes(qh[c].at[side], qh_s.at[c, side])
    wait_bytes(u1.at[0:7], u1_s)
    wait_bytes(u2.at[0:15], u2_s)
    wait_bytes(s3.at[0:3], s3_s)
    wait_bytes(s4.at[0:7], s4_s)
    wait_bytes(upd_v, out_sem.at[0])
    wait_bytes(mo_v, out_sem.at[1])


def hand_over(upd, mo, upd_out, mo_out, upd_v, mo_v, sem):
    pairs = ((mo, mo_v, mo_out), (upd, upd_v, upd_out))
    into = [pltpu.make_async_copy(src, held, sem.at[i]) for i, (src, held, _) in enumerate(pairs)]
    out = [pltpu.make_async_copy(held, dst, sem.at[2 + i]) for i, (_, held, dst) in enumerate(pairs)]
    for copy in into:
        copy.start()
    for before, after in zip(into, out):
        before.wait()
        after.start()
    for copy in out:
        copy.wait()


def on_device(activations, cotangent, momentum, kept_index):
    hbm = pl.BlockSpec(memory_space=pl.ANY)
    dma = pltpu.SemaphoreType.DMA
    vmem = pltpu.VMEM
    n = len(WIDTHS)
    out_shape = (jax.ShapeDtypeStruct((16, 4096), bf16), jax.ShapeDtypeStruct((16, 4096), f32))
    update, momentum_out = pl.pallas_call(
        kernel,
        name="outer_step",
        out_shape=out_shape,
        in_specs=[hbm] * 4,
        out_specs=(hbm, hbm),
        scratch_shapes=[
            pltpu.SMEM((8,), jnp.int32),
            vmem((128, 256), bf16),
            vmem((256, 4096), bf16),
            vmem((16, 4096), f32),
            vmem((512, 256), bf16),
            vmem((512, 1024), bf16),
            vmem((8, 128, 128), f32),
            vmem((8, 128, 128), f32),
            vmem((16, 8, 128), f32),
            vmem((16, 8, 128), f32),
            vmem((4, 8, 128), f32),
            vmem((8, 8, 128), f32),
            [vmem((16, 16, w), f32) for w in WIDTHS],
            [vmem((16, 16, w), jnp.int16) for w in WIDTHS],
            [vmem((12, 16, w), jnp.int16) for w in WIDTHS],
            [vmem((2, 2, 16, w), jnp.int16) for w in WIDTHS],
            vmem((n, 16, 1, 128), f32),
            vmem((n, 12, 1, 128), f32),
            vmem((n, 2, 2, 1, 128), f32),
            vmem((16, 4096), bf16),
            vmem((16, 4096), f32),
            dma((7,)),
            dma((2,)),
            dma((1 + n,)),
            dma((1 + n,)),
            *[dma] * 8,
            dma((n,)),
            dma((n,)),
            dma((n, 2)),
            dma((n, 2)),
            dma((n,)),
            dma((n,)),
            dma((n, 2)),
            dma((n, 2)),
            pltpu.SemaphoreType.REGULAR((2,)),
        ],
        compiler_params=pltpu.CompilerParams(
            collective_id=1, has_side_effects=True, vmem_limit_bytes=60 * 1024 * 1024
        ),
    )(kept_index, activations[0], cotangent[0], momentum[0])
    update, momentum_out = pl.pallas_call(
        hand_over,
        name="hand_over",
        out_shape=out_shape,
        in_specs=[hbm] * 2,
        out_specs=(hbm, hbm),
        scratch_shapes=[vmem((16, 4096), bf16), vmem((16, 4096), f32), dma((4,))],
        compiler_params=pltpu.CompilerParams(vmem_limit_bytes=60 * 1024 * 1024),
    )(update, momentum_out)
    return update, momentum_out[None]


def solution(mesh):
    return jax.shard_map(
        on_device,
        mesh=mesh,
        in_specs=(
            P("replica", "fsdp", None),
            P("replica", "fsdp", None),
            P("replica", "fsdp", None),
            P(),
        ),
        out_specs=(P("fsdp", None), P("replica", "fsdp", None)),
        check_vma=False,
    )
```

```python
import functools
import math

import jax
import jax.numpy as jnp
from jax import lax
from jax.experimental import pallas as pl
from jax.experimental.pallas import tpu as pltpu
from jax.sharding import PartitionSpec as P

MESH = pl.DeviceIdType.MESH
decay_rate = 0.999
f32, bf16 = jnp.float32, jnp.bfloat16
WIDTHS = (128, 384, 512)
STARTS = tuple(sum(WIDTHS[:c]) for c in range(len(WIDTHS)))
CHUNKS = range(len(WIDTHS))
ORDER = ('P0', 'U2', 'P1', 'A0', 'P2', 'S3', 'A1', 'S4', 'A2', 'X', 'M0', 'M1', 'UP', 'M2')


def halves(value):
    high = value.astype(bf16)
    return high, (value - high.astype(f32)).astype(bf16)


def dot(a, b):
    return jnp.dot(a, b, preferred_element_type=f32)


def mix_rows(columns, value):
    wide = [jnp.concatenate([c] * (value.shape[-1] // 128), axis=1) for c in columns]
    return functools.reduce(jnp.add, [w * value[..., i:i + 1, :] for i, w in enumerate(wide)])


def iota(shape, dim):
    return lax.broadcasted_iota(jnp.int32, shape, dim)


def wait_bytes(ref, sem):
    pltpu.make_async_copy(ref, ref, sem).wait()


def cosine_table():
    u = iota((8, 128), 0)
    angle = ((2 * (iota((8, 128), 1) & 7) + 1) * u) & 31
    value = jnp.zeros((8, 128), f32)
    for m in range(32):
        value = jnp.where(angle == m, math.cos(math.pi * m / 16), value)
    return jnp.where(u == 0, math.sqrt(1.0 / 8.0), 0.5 * value)


def kernel(kept_hbm, act, cot, mom, upd, mo, kept, a_own, c_own, m_in, a_in, c_in, u1, u1r, u2, u2r, s3, s4,
           g, q, qr, qh, sc, scr, sch, upd_v, mo_v, local_sem, out_sem, xs, xr, u1_s, u1_r, u2_s, u2_r, s3_s, s3_r,
           s4_s, s4_r, q_s, q_r, qh_s, qh_r, sc_s, sc_r, sch_s, sch_r, relay):
    r, f = lax.axis_index("replica"), lax.axis_index("fsdp")
    zl, yc, h, x = r // 8, r % 8, f // 4, f % 4
    own_rows = pl.ds(pl.multiple_of(x * 128, 128), 128)
    local = [
        pltpu.make_async_copy(kept_hbm, kept, local_sem.at[0]),
        pltpu.make_async_copy(act, a_own, local_sem.at[1]),
        pltpu.make_async_copy(cot, c_own.at[0:128], local_sem.at[2]),
        pltpu.make_async_copy(cot, c_own.at[128:256], local_sem.at[3]),
        pltpu.make_async_copy(mom, m_in, local_sem.at[4]),
        pltpu.make_async_copy(act, a_in.at[own_rows], local_sem.at[5]),
        pltpu.make_async_copy(cot.at[:, pl.ds(pl.multiple_of(x * 1024, 1024), 1024)], c_in.at[own_rows], local_sem.at[6]),
    ]

    def signal(sem, who):
        pl.semaphore_signal(sem, inc=1, device_id=who, device_id_type=MESH)

    def send(src, dst, ssem, rsem, who):
        pltpu.make_async_remote_copy(
            src_ref=src, dst_ref=dst, send_sem=ssem, recv_sem=rsem, device_id=who, device_id_type=MESH
        ).start()

    def fsdp_peer(d):
        return (r, (f + d) % 16)

    def x_peer(d):
        return (r, h * 4 + (x + d) % 4)

    def h_peer(d):
        return (r, ((h + d) % 4) * 4 + x)

    def yc_peer(d):
        return (zl * 8 + (yc + d) % 8, f)

    def z_peer(d):
        return (((zl + d) % 4) * 8 + yc, f)

    barrier = pltpu.get_barrier_semaphore()
    for d in (1, 3):
        signal(barrier, h_peer(d))
    for d in (2, 1, 3):
        signal(barrier, z_peer(d))
        signal(barrier, x_peer(d))

    @pl.loop(1, 8)
    def _(d):
        signal(barrier, yc_peer(d))

    for copy in local:
        copy.start()

    table = cosine_table()
    local[0].wait()
    k_at = iota((8, 128), 0)
    number = jnp.zeros((8, 128), jnp.int32)
    for k in range(8):
        number = jnp.where(k_at == k, kept[k], number)
    row_freq, col_freq = number >> 3, number & 7
    cu = jnp.zeros((8, 128), f32)
    cv = jnp.zeros((8, 128), f32)
    for u in range(8):
        line = jnp.broadcast_to(table[u:u + 1, :], (8, 128))
        cu = jnp.where(row_freq == u, line, cu)
        cv = jnp.where(col_freq == u, line, cv)
    cv512 = jnp.concatenate([cv] * 4, axis=1)
    row_at = iota((256, 256), 0)
    row_block = ((row_at >> 3) & 15) * 2 + (row_at >> 7)
    cu_tall = jnp.concatenate([jnp.concatenate([cu] * 2, axis=1)] * 32, axis=0)
    left = jnp.where((iota((256, 256), 1) >> 3) == row_block, cu_tall, 0.0)
    gather = ((iota((512, 128), 0) >> 3) == iota((512, 128), 1)).astype(bf16)
    block_sum = ((iota((128, 128), 0) >> 3) == (iota((128, 128), 1) >> 3)).astype(bf16)
    encode_rows = [jnp.broadcast_to(cu[:, i:i + 1], (8, 128)) for i in range(8)]
    cu_turned = jnp.concatenate([cu] * 16, axis=0).T[:8, :8]
    decode_rows = [jnp.broadcast_to(cu_turned[:, k:k + 1], (8, 128)) for k in range(8)]

    def two_part(value, matrix):
        n = value.shape[0]
        both = dot(jnp.concatenate(halves(value), axis=0), matrix)
        return both[:n] + both[n:]

    pl.semaphore_wait(barrier, 15)
    for d in (1, 3):
        signal(relay.at[0], h_peer(d))
    for d in (1, 2, 3):
        signal(relay.at[0], x_peer(d))

    for d in (2, 1, 3):
        send(act, a_in.at[own_rows], xs.at[0], xr.at[0], x_peer(d))
    for c in CHUNKS:
        for d in (2, 1, 3):
            columns = pl.ds(pl.multiple_of(((x + d) % 4) * 1024 + STARTS[c], 128), WIDTHS[c])
            send(cot.at[:, columns], c_in.at[own_rows, pl.ds(STARTS[c], WIDTHS[c])], xs.at[1 + c], xr.at[1 + c], x_peer(d))

    left_high = left.astype(bf16)
    left_mid, left_low = halves(left - left_high.astype(f32))
    local[1].wait()
    own_t = a_own[...].astype(f32).T.astype(bf16)
    mixed_act = jnp.concatenate(halves(dot(left_high, own_t) + dot(left_mid, own_t) + dot(left_low, own_t)), axis=1)
    for at in (2, 3, 4):
        local[at].wait()

    @pl.loop(1, 9)
    def _(d):
        j = (yc + d) % 8
        columns = pl.ds(pl.multiple_of(j * 512, 512), 512)
        mix = dot(mixed_act, c_own[:, columns])
        rows = mix_rows(encode_rows, (m_in[:, columns] * decay_rate).reshape(2, 8, 512))
        mix = (jnp.concatenate([mix.reshape(32, 8, 512), rows], axis=0) * cv512[None]).reshape(272, 512)
        sums = two_part(mix, gather)
        u1[j] = sums[:128] + pltpu.roll(sums[128:256], 64, 1)
        at = pl.ds(pl.multiple_of(f * 8, 8), 8)
        u1[j, at, :] = u1[j, at, :] + sums[256:264] + pltpu.roll(sums[264:272], 64, 1)

        @pl.when(d < 8)
        def _():
            send(u1.at[j], u1r.at[yc], u1_s, u1_r, yc_peer(d))

    local[5].wait()
    wait_bytes(a_in.at[0:384], xr.at[0])
    act_t = a_in[...].astype(f32).T.astype(bf16)
    local[6].wait()
    pl.semaphore_wait(relay.at[0], 5)
    for d in (1, 2, 3):
        signal(relay.at[1], x_peer(d))

    up, down, across = (h + 1) % 4, (h + 3) % 4, (h + 2) % 4

    def quantize(c, at, grad):
        groups = WIDTHS[c] // 128
        size = jnp.abs(grad)
        size = functools.reduce(jnp.maximum, [size[:, :, 128 * i:128 * (i + 1)] for i in range(groups)])
        size = jnp.maximum(jnp.max(size, axis=1, keepdims=True), 1e-33)
        sc[c, at] = size * (1.0 / 32767.0)
        inverse = jnp.concatenate([32767.0 / size] * groups, axis=2)
        q[c][at] = jnp.round(grad * inverse).astype(jnp.int32).astype(jnp.int16)

    def restore(c, value, scale):
        return value.astype(jnp.int32).astype(f32) * jnp.concatenate([scale] * (WIDTHS[c] // 128), axis=-1)

    def send_block(c, hh, xx, slot):
        at, who = hh * 4 + xx, (r, hh * 4 + xx)
        send(sc.at[c, at], scr.at[c, slot], sc_s.at[c], sc_r.at[c], who)
        send(q[c].at[at], qr[c].at[slot], q_s.at[c], q_r.at[c], who)

    def products(c):
        wait_bytes(c_in.at[0:384, pl.ds(STARTS[c], WIDTHS[c])], xr.at[1 + c])
        grad = dot(act_t, c_in[:, STARTS[c]:STARTS[c] + WIDTHS[c]]).reshape(16, 16, WIDTHS[c])
        g[c][...] = grad

        def ready(first, count):
            at = pl.ds(first, count)
            quantize(c, at, g[c][at])

        ready(across * 4, 4)
        for side, hh in ((0, up), (1, down)):
            at, who = pl.ds(across * 4 + 2 * side, 2), (r, hh * 4 + x)
            send(sc.at[c, at], sch.at[c, side], sch_s.at[c, side], sch_r.at[c, side], who)
            send(q[c].at[at], qh[c].at[side], qh_s.at[c, side], qh_r.at[c, side], who)
        ready(up * 4 + 2, 2)
        ready(down * 4, 2)
        for xx in (2, 3):
            send_block(c, up, xx, x)
            send_block(c, down, xx - 2, 4 + x)
        ready(h * 4, 4)
        qr[c][pl.ds(8 + x, 1)] = q[c][pl.ds(f, 1)]
        scr[c, pl.ds(8 + x, 1)] = sc[c, pl.ds(f, 1)]

    def send_beside():
        for c in CHUNKS:
            for d in (2, 1, 3):
                send_block(c, h, (x + d) % 4, 8 + x)

    def send_sums(c):
        for side, hh in ((0, up), (1, down)):
            at = pl.ds(hh * 4 + 2 * side, 2)
            wait_bytes(sch.at[c, side], sch_r.at[c, side])
            wait_bytes(qh[c].at[side], qh_r.at[c, side])
            quantize(c, at, g[c][at] + restore(c, qh[c][side], sch[c, side]))
            for xx in (0, 1):
                send_block(c, hh, xx + 2 * side, 4 * side + x)

    def sum_fsdp():
        pl.semaphore_wait(relay.at[1], 3)
        u1r[pl.ds(yc, 1)] = u1[pl.ds(yc, 1)]
        wait_bytes(u1r.at[0:7], u1_r)
        u2[...] = functools.reduce(jnp.add, [u1r[i] for i in range(8)]).reshape(16, 8, 128)

        @pl.loop(1, 16)
        def _(d):
            who = fsdp_peer(d)
            send(u2.at[who[1]], u2r.at[f], u2_s, u2_r, who)

        u2r[pl.ds(f, 1)] = u2[pl.ds(f, 1)]

    def sum_z():
        wait_bytes(u2r.at[0:15], u2_r)
        s3[pl.ds(zl, 1)] = functools.reduce(jnp.add, [u2r[i] for i in range(16)])[None]
        for d in (2, 1, 3):
            send(s3.at[zl], s3.at[zl], s3_s, s3_r, z_peer(d))
    def gather_yc():
        wait_bytes(s3.at[0:3], s3_r)
        s4[pl.ds(yc, 1)] = functools.reduce(jnp.add, [s3[i] for i in range(4)])[None]

        @pl.loop(1, 8)
        def _(d):
            send(s4.at[yc], s4.at[yc], s4_s, s4_r, yc_peer(d))

    def new_momentum(c):
        width, groups = WIDTHS[c], WIDTHS[c] // 128
        wait_bytes(scr.at[c, 0:11], sc_r.at[c])
        wait_bytes(qr[c].at[0:11], q_r.at[c])
        strips = []
        for xx in range(4):
            start = 1024 * xx + STARTS[c]
            accrued = decay_rate * m_in[:, start:start + width]
            for slot in (xx, 4 + xx, 8 + xx):
                accrued = accrued + restore(c, qr[c][slot], scr[c, slot])
            strips.append(accrued)
        accrued = jnp.concatenate(strips, axis=1)
        weight = jnp.concatenate([cv] * (4 * groups), axis=1)[None]
        rows = (mix_rows(encode_rows, accrued.reshape(2, 8, 4 * width)) * weight).reshape(16, 4 * width)
        tall = jnp.concatenate([rows[:, 128 * g:128 * (g + 1)] for g in range(4 * groups)], axis=0)
        tall = two_part(tall, block_sum)
        rows = jnp.concatenate([tall[16 * g:16 * (g + 1)] for g in range(4 * groups)], axis=1)
        rows = rows.reshape(2, 8, 4 * width) * weight
        left_over = accrued - mix_rows(decode_rows, rows).reshape(16, 4 * width)
        for xx in range(4):
            start = 1024 * xx + STARTS[c]
            mo_v[:, start:start + width] = left_over[:, xx * width:(xx + 1) * width]
            strip = pl.ds(start, width)
            pltpu.make_async_copy(mo_v.at[:, strip], mo.at[:, strip], out_sem.at[1]).start()

    def update():
        wait_bytes(s4.at[0:7], s4_r)
        total = s4[...]
        power = jnp.sum(total * total, axis=1, keepdims=True)
        scaled = (total / jnp.sqrt(power * (1.0 / 64.0) + 1e-06)).reshape(64, 128)
        bands = []
        for p in range(2):
            spread = ((iota((128, 512), 1) >> 3) + 64 * p == iota((128, 512), 0)).astype(bf16)
            wide = two_part(scaled, spread).reshape(8, 8, 512) * cv512[None]
            bands.append(jnp.tanh(mix_rows(decode_rows, wide)))
        for j in range(8):
            upd_v[:, 512 * j:512 * (j + 1)] = jnp.concatenate([band[j] for band in bands], axis=0).astype(bf16)
        pltpu.make_async_copy(upd_v, upd, out_sem.at[0]).start()

    steps = {"U2": sum_fsdp, "S3": sum_z, "S4": gather_yc, "UP": update, "X": send_beside}
    steps |= {f"P{c}": functools.partial(products, c) for c in CHUNKS}
    steps |= {f"A{c}": functools.partial(send_sums, c) for c in CHUNKS}
    steps |= {f"M{c}": functools.partial(new_momentum, c) for c in CHUNKS}
    for step in ORDER:
        steps[step]()

    wait_bytes(a_in.at[0:384], xs.at[0])
    for c in CHUNKS:
        wait_bytes(c_in.at[0:384, pl.ds(STARTS[c], WIDTHS[c])], xs.at[1 + c])
        wait_bytes(sc.at[c, 0:11], sc_s.at[c])
        wait_bytes(q[c].at[0:11], q_s.at[c])
        for side in range(2):
            wait_bytes(sch.at[c, side], sch_s.at[c, side])
            wait_bytes(qh[c].at[side], qh_s.at[c, side])
    wait_bytes(u1.at[0:7], u1_s)
    wait_bytes(u2.at[0:15], u2_s)
    wait_bytes(s3.at[0:3], s3_s)
    wait_bytes(s4.at[0:7], s4_s)
    wait_bytes(upd_v, out_sem.at[0])
    wait_bytes(mo_v, out_sem.at[1])


def hand_over(upd, mo, upd_out, mo_out, upd_v, mo_v, sem):
    pairs = ((mo, mo_v, mo_out), (upd, upd_v, upd_out))
    into = [pltpu.make_async_copy(src, held, sem.at[i]) for i, (src, held, _) in enumerate(pairs)]
    out = [pltpu.make_async_copy(held, dst, sem.at[2 + i]) for i, (_, held, dst) in enumerate(pairs)]
    for copy in into:
        copy.start()
    for before, after in zip(into, out):
        before.wait()
        after.start()
    for copy in out:
        copy.wait()


def on_device(activations, cotangent, momentum, kept_index):
    hbm = pl.BlockSpec(memory_space=pl.ANY)
    dma = pltpu.SemaphoreType.DMA
    vmem = pltpu.VMEM
    n = len(WIDTHS)
    out_shape = (jax.ShapeDtypeStruct((16, 4096), bf16), jax.ShapeDtypeStruct((16, 4096), f32))
    update, momentum_out = pl.pallas_call(
        kernel,
        name="outer_step",
        out_shape=out_shape,
        in_specs=[hbm] * 4,
        out_specs=(hbm, hbm),
        scratch_shapes=[
            pltpu.SMEM((8,), jnp.int32),
            vmem((128, 256), bf16),
            vmem((256, 4096), bf16),
            vmem((16, 4096), f32),
            vmem((512, 256), bf16),
            vmem((512, 1024), bf16),
            vmem((8, 128, 128), f32),
            vmem((8, 128, 128), f32),
            vmem((16, 8, 128), f32),
            vmem((16, 8, 128), f32),
            vmem((4, 8, 128), f32),
            vmem((8, 8, 128), f32),
            [vmem((16, 16, w), f32) for w in WIDTHS],
            [vmem((16, 16, w), jnp.int16) for w in WIDTHS],
            [vmem((12, 16, w), jnp.int16) for w in WIDTHS],
            [vmem((2, 2, 16, w), jnp.int16) for w in WIDTHS],
            vmem((n, 16, 1, 128), f32),
            vmem((n, 12, 1, 128), f32),
            vmem((n, 2, 2, 1, 128), f32),
            vmem((16, 4096), bf16),
            vmem((16, 4096), f32),
            dma((7,)),
            dma((2,)),
            dma((1 + n,)),
            dma((1 + n,)),
            *[dma] * 8,
            dma((n,)),
            dma((n,)),
            dma((n, 2)),
            dma((n, 2)),
            dma((n,)),
            dma((n,)),
            dma((n, 2)),
            dma((n, 2)),
            pltpu.SemaphoreType.REGULAR((2,)),
        ],
        compiler_params=pltpu.CompilerParams(
            collective_id=1, has_side_effects=True, vmem_limit_bytes=60 * 1024 * 1024
        ),
    )(kept_index, activations[0], cotangent[0], momentum[0])
    update, momentum_out = pl.pallas_call(
        hand_over,
        name="hand_over",
        out_shape=out_shape,
        in_specs=[hbm] * 2,
        out_specs=(hbm, hbm),
        scratch_shapes=[vmem((16, 4096), bf16), vmem((16, 4096), f32), dma((4,))],
        compiler_params=pltpu.CompilerParams(vmem_limit_bytes=60 * 1024 * 1024),
    )(update, momentum_out)
    return update, momentum_out[None]


def solution(mesh):
    return jax.shard_map(
        on_device,
        mesh=mesh,
        in_specs=(
            P("replica", "fsdp", None),
            P("replica", "fsdp", None),
            P("replica", "fsdp", None),
            P(),
        ),
        out_specs=(P("fsdp", None), P("replica", "fsdp", None)),
        check_vma=False,
    )
```

```python
import functools
import math

import jax
import jax.numpy as jnp
from jax import lax
from jax.experimental import pallas as pl
from jax.experimental.pallas import tpu as pltpu
from jax.sharding import PartitionSpec as P

MESH = pl.DeviceIdType.MESH
decay_rate = 0.999
f32, bf16 = jnp.float32, jnp.bfloat16
WIDTHS = (128, 384, 512)
STARTS = tuple(sum(WIDTHS[:c]) for c in range(len(WIDTHS)))
CHUNKS = range(len(WIDTHS))
ORDER = ('P0', 'U2', 'P1', 'A0', 'P2', 'S3', 'A1', 'S4', 'A2', 'X', 'M0', 'M1', 'UP', 'M2')


def halves(value):
    high = value.astype(bf16)
    return high, (value - high.astype(f32)).astype(bf16)


def dot(a, b):
    return jnp.dot(a, b, preferred_element_type=f32)


def mix_rows(columns, value):
    wide = [jnp.concatenate([c] * (value.shape[-1] // 128), axis=1) for c in columns]
    return functools.reduce(jnp.add, [w * value[..., i:i + 1, :] for i, w in enumerate(wide)])


def iota(shape, dim):
    return lax.broadcasted_iota(jnp.int32, shape, dim)


def wait_bytes(ref, sem):
    pltpu.make_async_copy(ref, ref, sem).wait()


def cosine_table():
    u = iota((8, 128), 0)
    angle = ((2 * (iota((8, 128), 1) & 7) + 1) * u) & 31
    value = jnp.zeros((8, 128), f32)
    for m in range(32):
        value = jnp.where(angle == m, math.cos(math.pi * m / 16), value)
    return jnp.where(u == 0, math.sqrt(1.0 / 8.0), 0.5 * value)


def kernel(kept_hbm, act, cot, mom, upd, mo, kept, a_own, c_own, m_in, a_in, c_in, u1, u1r, u2, u2r, s3, s4,
           g, q, qr, qh, sc, scr, sch, upd_v, mo_v, local_sem, out_sem, xs, xr, u1_s, u1_r, u2_s, u2_r, s3_s, s3_r,
           s4_s, s4_r, q_s, q_r, qh_s, qh_r, sc_s, sc_r, sch_s, sch_r, relay):
    r, f = lax.axis_index("replica"), lax.axis_index("fsdp")
    zl, yc, h, x = r // 8, r % 8, f // 4, f % 4
    own_rows = pl.ds(pl.multiple_of(x * 128, 128), 128)
    local = [
        pltpu.make_async_copy(kept_hbm, kept, local_sem.at[0]),
        pltpu.make_async_copy(act, a_own, local_sem.at[1]),
        pltpu.make_async_copy(cot, c_own.at[0:128], local_sem.at[2]),
        pltpu.make_async_copy(cot, c_own.at[128:256], local_sem.at[3]),
        pltpu.make_async_copy(mom, m_in, local_sem.at[4]),
        pltpu.make_async_copy(act, a_in.at[own_rows], local_sem.at[5]),
        pltpu.make_async_copy(cot.at[:, pl.ds(pl.multiple_of(x * 1024, 1024), 1024)], c_in.at[own_rows], local_sem.at[6]),
    ]

    def signal(sem, who):
        pl.semaphore_signal(sem, inc=1, device_id=who, device_id_type=MESH)

    def send(src, dst, ssem, rsem, who):
        pltpu.make_async_remote_copy(
            src_ref=src, dst_ref=dst, send_sem=ssem, recv_sem=rsem, device_id=who, device_id_type=MESH
        ).start()

    def fsdp_peer(d):
        return (r, (f + d) % 16)

    def x_peer(d):
        return (r, h * 4 + (x + d) % 4)

    def h_peer(d):
        return (r, ((h + d) % 4) * 4 + x)

    def yc_peer(d):
        return (zl * 8 + (yc + d) % 8, f)

    def z_peer(d):
        return (((zl + d) % 4) * 8 + yc, f)

    barrier = pltpu.get_barrier_semaphore()
    for d in (1, 3):
        signal(barrier, h_peer(d))
    for d in (2, 1, 3):
        signal(barrier, z_peer(d))
        signal(barrier, x_peer(d))

    @pl.loop(1, 8)
    def _(d):
        signal(barrier, yc_peer(d))

    for copy in local:
        copy.start()

    table = cosine_table()
    local[0].wait()
    k_at = iota((8, 128), 0)
    number = jnp.zeros((8, 128), jnp.int32)
    for k in range(8):
        number = jnp.where(k_at == k, kept[k], number)
    row_freq, col_freq = number >> 3, number & 7
    cu = jnp.zeros((8, 128), f32)
    cv = jnp.zeros((8, 128), f32)
    for u in range(8):
        line = jnp.broadcast_to(table[u:u + 1, :], (8, 128))
        cu = jnp.where(row_freq == u, line, cu)
        cv = jnp.where(col_freq == u, line, cv)
    cv512 = jnp.concatenate([cv] * 4, axis=1)
    row_at = iota((256, 256), 0)
    row_block = ((row_at >> 3) & 15) * 2 + (row_at >> 7)
    cu_tall = jnp.concatenate([jnp.concatenate([cu] * 2, axis=1)] * 32, axis=0)
    left = jnp.where((iota((256, 256), 1) >> 3) == row_block, cu_tall, 0.0)
    gather = ((iota((512, 128), 0) >> 3) == iota((512, 128), 1)).astype(bf16)
    block_sum = ((iota((128, 128), 0) >> 3) == (iota((128, 128), 1) >> 3)).astype(bf16)
    encode_rows = [jnp.broadcast_to(cu[:, i:i + 1], (8, 128)) for i in range(8)]
    cu_turned = jnp.concatenate([cu] * 16, axis=0).T[:8, :8]
    decode_rows = [jnp.broadcast_to(cu_turned[:, k:k + 1], (8, 128)) for k in range(8)]

    def two_part(value, matrix):
        n = value.shape[0]
        both = dot(jnp.concatenate(halves(value), axis=0), matrix)
        return both[:n] + both[n:]

    pl.semaphore_wait(barrier, 15)
    for d in (1, 3):
        signal(relay.at[0], h_peer(d))
    for d in (1, 2, 3):
        signal(relay.at[0], x_peer(d))

    for d in (2, 1, 3):
        send(act, a_in.at[own_rows], xs.at[0], xr.at[0], x_peer(d))
    for c in CHUNKS:
        for d in (2, 1, 3):
            columns = pl.ds(pl.multiple_of(((x + d) % 4) * 1024 + STARTS[c], 128), WIDTHS[c])
            send(cot.at[:, columns], c_in.at[own_rows, pl.ds(STARTS[c], WIDTHS[c])], xs.at[1 + c], xr.at[1 + c], x_peer(d))

    left_high = left.astype(bf16)
    left_mid, left_low = halves(left - left_high.astype(f32))
    local[1].wait()
    own_t = a_own[...].astype(f32).T.astype(bf16)
    mixed_act = jnp.concatenate(halves(dot(left_high, own_t) + dot(left_mid, own_t) + dot(left_low, own_t)), axis=1)
    for at in (2, 3, 4):
        local[at].wait()

    def folded(j):
        columns = pl.ds(pl.multiple_of(j * 512, 512), 512)
        mix = dot(mixed_act, c_own[:, columns])
        rows = mix_rows(encode_rows, (m_in[:, columns] * decay_rate).reshape(2, 8, 512))
        mix = (jnp.concatenate([mix.reshape(32, 8, 512), rows], axis=0) * cv512[None]).reshape(272, 512)
        return two_part(mix, gather)

    @pl.loop(0, 4)
    def _(i):
        pair = [(yc + 2 * i + 1) % 8, (yc + 2 * i + 2) % 8]
        at = pl.ds(pl.multiple_of(f * 8, 8), 8)
        for j, sums in zip(pair, [folded(j) for j in pair]):
            u1[j] = sums[:128] + pltpu.roll(sums[128:256], 64, 1)
            u1[j, at, :] = u1[j, at, :] + sums[256:264] + pltpu.roll(sums[264:272], 64, 1)
        send(u1.at[pair[0]], u1r.at[yc], u1_s, u1_r, yc_peer(2 * i + 1))

        @pl.when(i < 3)
        def _():
            send(u1.at[pair[1]], u1r.at[yc], u1_s, u1_r, yc_peer(2 * i + 2))

    pl.semaphore_wait(relay.at[0], 5)
    for d in (1, 2, 3):
        signal(relay.at[1], x_peer(d))

    local[5].wait()
    wait_bytes(a_in.at[0:384], xr.at[0])
    act_t = a_in[...].astype(f32).T.astype(bf16)
    local[6].wait()

    up, down, across = (h + 1) % 4, (h + 3) % 4, (h + 2) % 4

    def quantize(c, at, grad):
        groups = WIDTHS[c] // 128
        size = jnp.abs(grad)
        size = functools.reduce(jnp.maximum, [size[:, :, 128 * i:128 * (i + 1)] for i in range(groups)])
        size = jnp.maximum(jnp.max(size, axis=1, keepdims=True), 1e-33)
        sc[c, at] = size * (1.0 / 32767.0)
        inverse = jnp.concatenate([32767.0 / size] * groups, axis=2)
        q[c][at] = jnp.round(grad * inverse).astype(jnp.int32).astype(jnp.int16)

    def restore(c, value, scale):
        return value.astype(jnp.int32).astype(f32) * jnp.concatenate([scale] * (WIDTHS[c] // 128), axis=-1)

    def send_block(c, hh, xx, slot):
        at, who = hh * 4 + xx, (r, hh * 4 + xx)
        send(sc.at[c, at], scr.at[c, slot], sc_s.at[c], sc_r.at[c], who)
        send(q[c].at[at], qr[c].at[slot], q_s.at[c], q_r.at[c], who)

    def products(c):
        wait_bytes(c_in.at[0:384, pl.ds(STARTS[c], WIDTHS[c])], xr.at[1 + c])
        grad = dot(act_t, c_in[:, STARTS[c]:STARTS[c] + WIDTHS[c]]).reshape(16, 16, WIDTHS[c])
        g[c][...] = grad
        quantize(c, slice(None), grad)
        for side, hh in ((0, up), (1, down)):
            at, who = pl.ds(across * 4 + 2 * side, 2), (r, hh * 4 + x)
            send(sc.at[c, at], sch.at[c, side], sch_s.at[c, side], sch_r.at[c, side], who)
            send(q[c].at[at], qh[c].at[side], qh_s.at[c, side], qh_r.at[c, side], who)
        for xx in (2, 3):
            send_block(c, up, xx, x)
            send_block(c, down, xx - 2, 4 + x)
        qr[c][pl.ds(8 + x, 1)] = q[c][pl.ds(f, 1)]
        scr[c, pl.ds(8 + x, 1)] = sc[c, pl.ds(f, 1)]

    def send_beside():
        for c in CHUNKS:
            for d in (2, 1, 3):
                send_block(c, h, (x + d) % 4, 8 + x)

    def send_sums(c):
        for side, hh in ((0, up), (1, down)):
            at = pl.ds(hh * 4 + 2 * side, 2)
            wait_bytes(sch.at[c, side], sch_r.at[c, side])
            wait_bytes(qh[c].at[side], qh_r.at[c, side])
            quantize(c, at, g[c][at] + restore(c, qh[c][side], sch[c, side]))
            for xx in (0, 1):
                send_block(c, hh, xx + 2 * side, 4 * side + x)

    def sum_fsdp():
        pl.semaphore_wait(relay.at[1], 3)
        u1r[pl.ds(yc, 1)] = u1[pl.ds(yc, 1)]
        wait_bytes(u1r.at[0:7], u1_r)
        u2[...] = functools.reduce(jnp.add, [u1r[i] for i in range(8)]).reshape(16, 8, 128)

        @pl.loop(1, 16)
        def _(d):
            who = fsdp_peer(d)
            send(u2.at[who[1]], u2r.at[f], u2_s, u2_r, who)

        u2r[pl.ds(f, 1)] = u2[pl.ds(f, 1)]

    def sum_z():
        wait_bytes(u2r.at[0:15], u2_r)
        s3[pl.ds(zl, 1)] = functools.reduce(jnp.add, [u2r[i] for i in range(16)])[None]
        for d in (2, 1, 3):
            send(s3.at[zl], s3.at[zl], s3_s, s3_r, z_peer(d))
    def gather_yc():
        wait_bytes(s3.at[0:3], s3_r)
        s4[pl.ds(yc, 1)] = functools.reduce(jnp.add, [s3[i] for i in range(4)])[None]

        @pl.loop(1, 8)
        def _(d):
            send(s4.at[yc], s4.at[yc], s4_s, s4_r, yc_peer(d))

    def new_momentum(c):
        width, groups = WIDTHS[c], WIDTHS[c] // 128
        wait_bytes(scr.at[c, 0:11], sc_r.at[c])
        wait_bytes(qr[c].at[0:11], q_r.at[c])
        strips = []
        for xx in range(4):
            start = 1024 * xx + STARTS[c]
            accrued = decay_rate * m_in[:, start:start + width]
            for slot in (xx, 4 + xx, 8 + xx):
                accrued = accrued + restore(c, qr[c][slot], scr[c, slot])
            strips.append(accrued)
        accrued = jnp.concatenate(strips, axis=1)
        weight = jnp.concatenate([cv] * (4 * groups), axis=1)[None]
        rows = (mix_rows(encode_rows, accrued.reshape(2, 8, 4 * width)) * weight).reshape(16, 4 * width)
        tall = jnp.concatenate([rows[:, 128 * g:128 * (g + 1)] for g in range(4 * groups)], axis=0)
        tall = two_part(tall, block_sum)
        rows = jnp.concatenate([tall[16 * g:16 * (g + 1)] for g in range(4 * groups)], axis=1)
        rows = rows.reshape(2, 8, 4 * width) * weight
        left_over = accrued - mix_rows(decode_rows, rows).reshape(16, 4 * width)
        for xx in range(4):
            start = 1024 * xx + STARTS[c]
            mo_v[:, start:start + width] = left_over[:, xx * width:(xx + 1) * width]
            strip = pl.ds(start, width)
            pltpu.make_async_copy(mo_v.at[:, strip], mo.at[:, strip], out_sem.at[1]).start()

    def update():
        wait_bytes(s4.at[0:7], s4_r)
        total = s4[...]
        power = jnp.sum(total * total, axis=1, keepdims=True)
        scaled = (total / jnp.sqrt(power * (1.0 / 64.0) + 1e-06)).reshape(64, 128)
        bands = []
        for p in range(2):
            spread = ((iota((128, 512), 1) >> 3) + 64 * p == iota((128, 512), 0)).astype(bf16)
            wide = two_part(scaled, spread).reshape(8, 8, 512) * cv512[None]
            bands.append(jnp.tanh(mix_rows(decode_rows, wide)))
        for j in range(8):
            upd_v[:, 512 * j:512 * (j + 1)] = jnp.concatenate([band[j] for band in bands], axis=0).astype(bf16)
        pltpu.make_async_copy(upd_v, upd, out_sem.at[0]).start()

    steps = {"U2": sum_fsdp, "S3": sum_z, "S4": gather_yc, "UP": update, "X": send_beside}
    steps |= {f"P{c}": functools.partial(products, c) for c in CHUNKS}
    steps |= {f"A{c}": functools.partial(send_sums, c) for c in CHUNKS}
    steps |= {f"M{c}": functools.partial(new_momentum, c) for c in CHUNKS}
    for step in ORDER:
        steps[step]()

    wait_bytes(a_in.at[0:384], xs.at[0])
    for c in CHUNKS:
        wait_bytes(c_in.at[0:384, pl.ds(STARTS[c], WIDTHS[c])], xs.at[1 + c])
        wait_bytes(sc.at[c, 0:11], sc_s.at[c])
        wait_bytes(q[c].at[0:11], q_s.at[c])
        for side in range(2):
            wait_bytes(sch.at[c, side], sch_s.at[c, side])
            wait_bytes(qh[c].at[side], qh_s.at[c, side])
    wait_bytes(u1.at[0:7], u1_s)
    wait_bytes(u2.at[0:15], u2_s)
    wait_bytes(s3.at[0:3], s3_s)
    wait_bytes(s4.at[0:7], s4_s)
    wait_bytes(upd_v, out_sem.at[0])
    wait_bytes(mo_v, out_sem.at[1])


def hand_over(upd, mo, upd_out, mo_out, upd_v, mo_v, sem):
    pairs = ((mo, mo_v, mo_out), (upd, upd_v, upd_out))
    into = [pltpu.make_async_copy(src, held, sem.at[i]) for i, (src, held, _) in enumerate(pairs)]
    out = [pltpu.make_async_copy(held, dst, sem.at[2 + i]) for i, (_, held, dst) in enumerate(pairs)]
    for copy in into:
        copy.start()
    for before, after in zip(into, out):
        before.wait()
        after.start()
    for copy in out:
        copy.wait()


def on_device(activations, cotangent, momentum, kept_index):
    hbm = pl.BlockSpec(memory_space=pl.ANY)
    dma = pltpu.SemaphoreType.DMA
    vmem = pltpu.VMEM
    n = len(WIDTHS)
    out_shape = (jax.ShapeDtypeStruct((16, 4096), bf16), jax.ShapeDtypeStruct((16, 4096), f32))
    update, momentum_out = pl.pallas_call(
        kernel,
        name="outer_step",
        out_shape=out_shape,
        in_specs=[hbm] * 4,
        out_specs=(hbm, hbm),
        scratch_shapes=[
            pltpu.SMEM((8,), jnp.int32),
            vmem((128, 256), bf16),
            vmem((256, 4096), bf16),
            vmem((16, 4096), f32),
            vmem((512, 256), bf16),
            vmem((512, 1024), bf16),
            vmem((8, 128, 128), f32),
            vmem((8, 128, 128), f32),
            vmem((16, 8, 128), f32),
            vmem((16, 8, 128), f32),
            vmem((4, 8, 128), f32),
            vmem((8, 8, 128), f32),
            [vmem((16, 16, w), f32) for w in WIDTHS],
            [vmem((16, 16, w), jnp.int16) for w in WIDTHS],
            [vmem((12, 16, w), jnp.int16) for w in WIDTHS],
            [vmem((2, 2, 16, w), jnp.int16) for w in WIDTHS],
            vmem((n, 16, 1, 128), f32),
            vmem((n, 12, 1, 128), f32),
            vmem((n, 2, 2, 1, 128), f32),
            vmem((16, 4096), bf16),
            vmem((16, 4096), f32),
            dma((7,)),
            dma((2,)),
            dma((1 + n,)),
            dma((1 + n,)),
            *[dma] * 8,
            dma((n,)),
            dma((n,)),
            dma((n, 2)),
            dma((n, 2)),
            dma((n,)),
            dma((n,)),
            dma((n, 2)),
            dma((n, 2)),
            pltpu.SemaphoreType.REGULAR((2,)),
        ],
        compiler_params=pltpu.CompilerParams(
            collective_id=1, has_side_effects=True, vmem_limit_bytes=60 * 1024 * 1024
        ),
    )(kept_index, activations[0], cotangent[0], momentum[0])
    update, momentum_out = pl.pallas_call(
        hand_over,
        name="hand_over",
        out_shape=out_shape,
        in_specs=[hbm] * 2,
        out_specs=(hbm, hbm),
        scratch_shapes=[vmem((16, 4096), bf16), vmem((16, 4096), f32), dma((4,))],
        compiler_params=pltpu.CompilerParams(vmem_limit_bytes=60 * 1024 * 1024),
    )(update, momentum_out)
    return update, momentum_out[None]


def solution(mesh):
    return jax.shard_map(
        on_device,
        mesh=mesh,
        in_specs=(
            P("replica", "fsdp", None),
            P("replica", "fsdp", None),
            P("replica", "fsdp", None),
            P(),
        ),
        out_specs=(P("fsdp", None), P("replica", "fsdp", None)),
        check_vma=False,
    )
```

```python
import functools
import math

import jax
import jax.numpy as jnp
from jax import lax
from jax.experimental import pallas as pl
from jax.experimental.pallas import tpu as pltpu
from jax.sharding import PartitionSpec as P

MESH = pl.DeviceIdType.MESH
decay_rate = 0.999
f32, bf16 = jnp.float32, jnp.bfloat16
WIDTHS = (128, 384, 512)
STARTS = tuple(sum(WIDTHS[:c]) for c in range(len(WIDTHS)))
CHUNKS = range(len(WIDTHS))
ORDER = ('P0', 'U2', 'P1', 'A0', 'P2', 'S3', 'A1', 'S4', 'A2', 'X', 'M0', 'M1', 'UP', 'M2')


def halves(value):
    high = value.astype(bf16)
    return high, (value - high.astype(f32)).astype(bf16)


def dot(a, b):
    return jnp.dot(a, b, preferred_element_type=f32)


def mix_rows(columns, value):
    wide = [jnp.concatenate([c] * (value.shape[-1] // 128), axis=1) for c in columns]
    return functools.reduce(jnp.add, [w * value[..., i:i + 1, :] for i, w in enumerate(wide)])


def iota(shape, dim):
    return lax.broadcasted_iota(jnp.int32, shape, dim)


def wait_bytes(ref, sem):
    pltpu.make_async_copy(ref, ref, sem).wait()


def cosine_table():
    u = iota((8, 128), 0)
    angle = ((2 * (iota((8, 128), 1) & 7) + 1) * u) & 31
    value = jnp.zeros((8, 128), f32)
    for m in range(32):
        value = jnp.where(angle == m, math.cos(math.pi * m / 16), value)
    return jnp.where(u == 0, math.sqrt(1.0 / 8.0), 0.5 * value)


def kernel(kept_hbm, act, cot, mom, upd, mo, kept, a_own, c_own, m_in, a_in, c_in, u1, u1r, u2, u2r, s3, s4,
           g, q, qr, qh, sc, scr, sch, upd_v, mo_v, local_sem, out_sem, xs, xr, u1_s, u1_r, u2_s, u2_r, s3_s, s3_r,
           s4_s, s4_r, q_s, q_r, qh_s, qh_r, sc_s, sc_r, sch_s, sch_r, relay):
    r, f = lax.axis_index("replica"), lax.axis_index("fsdp")
    zl, yc, h, x = r // 8, r % 8, f // 4, f % 4
    own_rows = pl.ds(pl.multiple_of(x * 128, 128), 128)
    local = [
        pltpu.make_async_copy(kept_hbm, kept, local_sem.at[0]),
        pltpu.make_async_copy(act, a_own, local_sem.at[1]),
        pltpu.make_async_copy(cot, c_own.at[0:128], local_sem.at[2]),
        pltpu.make_async_copy(cot, c_own.at[128:256], local_sem.at[3]),
        pltpu.make_async_copy(mom, m_in, local_sem.at[4]),
        pltpu.make_async_copy(act, a_in.at[own_rows], local_sem.at[5]),
        pltpu.make_async_copy(cot.at[:, pl.ds(pl.multiple_of(x * 1024, 1024), 1024)], c_in.at[own_rows], local_sem.at[6]),
    ]

    def signal(sem, who):
        pl.semaphore_signal(sem, inc=1, device_id=who, device_id_type=MESH)

    def send(src, dst, ssem, rsem, who):
        pltpu.make_async_remote_copy(
            src_ref=src, dst_ref=dst, send_sem=ssem, recv_sem=rsem, device_id=who, device_id_type=MESH
        ).start()

    def fsdp_peer(d):
        return (r, (f + d) % 16)

    def x_peer(d):
        return (r, h * 4 + (x + d) % 4)

    def h_peer(d):
        return (r, ((h + d) % 4) * 4 + x)

    def yc_peer(d):
        return (zl * 8 + (yc + d) % 8, f)

    def z_peer(d):
        return (((zl + d) % 4) * 8 + yc, f)

    barrier = pltpu.get_barrier_semaphore()
    for d in (1, 3):
        signal(barrier, h_peer(d))
    for d in (2, 1, 3):
        signal(barrier, z_peer(d))
        signal(barrier, x_peer(d))

    @pl.loop(1, 8)
    def _(d):
        signal(barrier, yc_peer(d))

    for copy in local:
        copy.start()

    table = cosine_table()
    local[0].wait()
    k_at = iota((8, 128), 0)
    number = jnp.zeros((8, 128), jnp.int32)
    for k in range(8):
        number = jnp.where(k_at == k, kept[k], number)
    row_freq, col_freq = number >> 3, number & 7
    cu = jnp.zeros((8, 128), f32)
    cv = jnp.zeros((8, 128), f32)
    for u in range(8):
        line = jnp.broadcast_to(table[u:u + 1, :], (8, 128))
        cu = jnp.where(row_freq == u, line, cu)
        cv = jnp.where(col_freq == u, line, cv)
    cv512 = jnp.concatenate([cv] * 4, axis=1)
    row_at = iota((256, 256), 0)
    row_block = ((row_at >> 3) & 15) * 2 + (row_at >> 7)
    cu_tall = jnp.concatenate([jnp.concatenate([cu] * 2, axis=1)] * 32, axis=0)
    left = jnp.where((iota((256, 256), 1) >> 3) == row_block, cu_tall, 0.0)
    gather = ((iota((512, 128), 0) >> 3) == iota((512, 128), 1)).astype(bf16)
    block_sum = ((iota((128, 128), 0) >> 3) == (iota((128, 128), 1) >> 3)).astype(bf16)
    encode_rows = [jnp.broadcast_to(cu[:, i:i + 1], (8, 128)) for i in range(8)]
    cu_turned = jnp.concatenate([cu] * 16, axis=0).T[:8, :8]
    decode_rows = [jnp.broadcast_to(cu_turned[:, k:k + 1], (8, 128)) for k in range(8)]

    def two_part(value, matrix):
        n = value.shape[0]
        both = dot(jnp.concatenate(halves(value), axis=0), matrix)
        return both[:n] + both[n:]

    pl.semaphore_wait(barrier, 15)
    for d in (1, 3):
        signal(relay.at[0], h_peer(d))
    for d in (1, 2, 3):
        signal(relay.at[0], x_peer(d))

    for d in (2, 1, 3):
        send(act, a_in.at[own_rows], xs.at[0], xr.at[0], x_peer(d))
    for c in CHUNKS:
        for d in (2, 1, 3):
            columns = pl.ds(pl.multiple_of(((x + d) % 4) * 1024 + STARTS[c], 128), WIDTHS[c])
            send(cot.at[:, columns], c_in.at[own_rows, pl.ds(STARTS[c], WIDTHS[c])], xs.at[1 + c], xr.at[1 + c], x_peer(d))

    left_high = left.astype(bf16)
    left_mid, left_low = halves(left - left_high.astype(f32))
    local[1].wait()
    own_t = a_own[...].astype(f32).T.astype(bf16)
    mixed_act = jnp.concatenate(halves(dot(left_high, own_t) + dot(left_mid, own_t) + dot(left_low, own_t)), axis=1)
    for at in (2, 3, 4):
        local[at].wait()

    def folded(j):
        columns = pl.ds(pl.multiple_of(j * 512, 512), 512)
        mix = dot(mixed_act, c_own[:, columns])
        rows = mix_rows(encode_rows, (m_in[:, columns] * decay_rate).reshape(2, 8, 512))
        mix = (jnp.concatenate([mix.reshape(32, 8, 512), rows], axis=0) * cv512[None]).reshape(272, 512)
        return two_part(mix, gather)

    @pl.loop(0, 4)
    def _(i):
        pair = [(yc + 2 * i + 1) % 8, (yc + 2 * i + 2) % 8]
        at = pl.ds(pl.multiple_of(f * 8, 8), 8)
        for j, sums in zip(pair, [folded(j) for j in pair]):
            u1[j] = sums[:128] + pltpu.roll(sums[128:256], 64, 1)
            u1[j, at, :] = u1[j, at, :] + sums[256:264] + pltpu.roll(sums[264:272], 64, 1)
        send(u1.at[pair[0]], u1r.at[yc], u1_s, u1_r, yc_peer(2 * i + 1))

        @pl.when(i < 3)
        def _():
            send(u1.at[pair[1]], u1r.at[yc], u1_s, u1_r, yc_peer(2 * i + 2))

    local[5].wait()
    wait_bytes(a_in.at[0:384], xr.at[0])
    act_t = a_in[...].astype(f32).T.astype(bf16)
    local[6].wait()
    pl.semaphore_wait(relay.at[0], 5)
    for d in (1, 2, 3):
        signal(relay.at[1], x_peer(d))

    up, down, across = (h + 1) % 4, (h + 3) % 4, (h + 2) % 4

    def quantize(c, at, grad):
        groups = WIDTHS[c] // 128
        size = jnp.abs(grad)
        size = functools.reduce(jnp.maximum, [size[:, :, 128 * i:128 * (i + 1)] for i in range(groups)])
        size = jnp.maximum(jnp.max(size, axis=1, keepdims=True), 1e-33)
        sc[c, at] = size * (1.0 / 32767.0)
        inverse = jnp.concatenate([32767.0 / size] * groups, axis=2)
        q[c][at] = jnp.round(grad * inverse).astype(jnp.int32).astype(jnp.int16)

    def restore(c, value, scale):
        return value.astype(jnp.int32).astype(f32) * jnp.concatenate([scale] * (WIDTHS[c] // 128), axis=-1)

    def send_block(c, hh, xx, slot):
        at, who = hh * 4 + xx, (r, hh * 4 + xx)
        send(sc.at[c, at], scr.at[c, slot], sc_s.at[c], sc_r.at[c], who)
        send(q[c].at[at], qr[c].at[slot], q_s.at[c], q_r.at[c], who)

    def products(c):
        wait_bytes(c_in.at[0:384, pl.ds(STARTS[c], WIDTHS[c])], xr.at[1 + c])
        grad = dot(act_t, c_in[:, STARTS[c]:STARTS[c] + WIDTHS[c]]).reshape(16, 16, WIDTHS[c])
        g[c][...] = grad

        def ready(first, count):
            at = pl.ds(first, count)
            quantize(c, at, g[c][at])

        ready(across * 4, 4)
        for side, hh in ((0, up), (1, down)):
            at, who = pl.ds(across * 4 + 2 * side, 2), (r, hh * 4 + x)
            send(sc.at[c, at], sch.at[c, side], sch_s.at[c, side], sch_r.at[c, side], who)
            send(q[c].at[at], qh[c].at[side], qh_s.at[c, side], qh_r.at[c, side], who)
        ready(up * 4 + 2, 2)
        ready(down * 4, 2)
        for xx in (2, 3):
            send_block(c, up, xx, x)
            send_block(c, down, xx - 2, 4 + x)
        ready(h * 4, 4)
        qr[c][pl.ds(8 + x, 1)] = q[c][pl.ds(f, 1)]
        scr[c, pl.ds(8 + x, 1)] = sc[c, pl.ds(f, 1)]

    def send_beside():
        for c in CHUNKS:
            for d in (2, 1, 3):
                send_block(c, h, (x + d) % 4, 8 + x)

    def send_sums(c):
        for side, hh in ((0, up), (1, down)):
            at = pl.ds(hh * 4 + 2 * side, 2)
            wait_bytes(sch.at[c, side], sch_r.at[c, side])
            wait_bytes(qh[c].at[side], qh_r.at[c, side])
            quantize(c, at, g[c][at] + restore(c, qh[c][side], sch[c, side]))
            for xx in (0, 1):
                send_block(c, hh, xx + 2 * side, 4 * side + x)

    def sum_fsdp():
        pl.semaphore_wait(relay.at[1], 3)
        u1r[pl.ds(yc, 1)] = u1[pl.ds(yc, 1)]
        wait_bytes(u1r.at[0:7], u1_r)
        u2[...] = functools.reduce(jnp.add, [u1r[i] for i in range(8)]).reshape(16, 8, 128)

        @pl.loop(1, 16)
        def _(d):
            who = fsdp_peer(d)
            send(u2.at[who[1]], u2r.at[f], u2_s, u2_r, who)

        u2r[pl.ds(f, 1)] = u2[pl.ds(f, 1)]

    def sum_z():
        wait_bytes(u2r.at[0:15], u2_r)
        s3[pl.ds(zl, 1)] = functools.reduce(jnp.add, [u2r[i] for i in range(16)])[None]
        for d in (2, 1, 3):
            send(s3.at[zl], s3.at[zl], s3_s, s3_r, z_peer(d))
    def gather_yc():
        wait_bytes(s3.at[0:3], s3_r)
        s4[pl.ds(yc, 1)] = functools.reduce(jnp.add, [s3[i] for i in range(4)])[None]

        @pl.loop(1, 8)
        def _(d):
            send(s4.at[yc], s4.at[yc], s4_s, s4_r, yc_peer(d))

    def new_momentum(c):
        width, groups = WIDTHS[c], WIDTHS[c] // 128
        wait_bytes(scr.at[c, 0:11], sc_r.at[c])
        wait_bytes(qr[c].at[0:11], q_r.at[c])
        strips = []
        for xx in range(4):
            start = 1024 * xx + STARTS[c]
            accrued = decay_rate * m_in[:, start:start + width]
            for slot in (xx, 4 + xx, 8 + xx):
                accrued = accrued + restore(c, qr[c][slot], scr[c, slot])
            strips.append(accrued)
        accrued = jnp.concatenate(strips, axis=1)
        weight = jnp.concatenate([cv] * (4 * groups), axis=1)[None]
        rows = (mix_rows(encode_rows, accrued.reshape(2, 8, 4 * width)) * weight).reshape(16, 4 * width)
        tall = jnp.concatenate([rows[:, 128 * g:128 * (g + 1)] for g in range(4 * groups)], axis=0)
        tall = two_part(tall, block_sum)
        rows = jnp.concatenate([tall[16 * g:16 * (g + 1)] for g in range(4 * groups)], axis=1)
        rows = rows.reshape(2, 8, 4 * width) * weight
        left_over = accrued - mix_rows(decode_rows, rows).reshape(16, 4 * width)
        for xx in range(4):
            start = 1024 * xx + STARTS[c]
            mo_v[:, start:start + width] = left_over[:, xx * width:(xx + 1) * width]
            strip = pl.ds(start, width)
            pltpu.make_async_copy(mo_v.at[:, strip], mo.at[:, strip], out_sem.at[1]).start()

    def update():
        wait_bytes(s4.at[0:7], s4_r)
        total = s4[...]
        power = jnp.sum(total * total, axis=1, keepdims=True)
        scaled = (total / jnp.sqrt(power * (1.0 / 64.0) + 1e-06)).reshape(64, 128)
        bands = []
        for p in range(2):
            spread = ((iota((128, 512), 1) >> 3) + 64 * p == iota((128, 512), 0)).astype(bf16)
            wide = two_part(scaled, spread).reshape(8, 8, 512) * cv512[None]
            bands.append(jnp.tanh(mix_rows(decode_rows, wide)))
        for j in range(8):
            upd_v[:, 512 * j:512 * (j + 1)] = jnp.concatenate([band[j] for band in bands], axis=0).astype(bf16)
        pltpu.make_async_copy(upd_v, upd, out_sem.at[0]).start()

    steps = {"U2": sum_fsdp, "S3": sum_z, "S4": gather_yc, "UP": update, "X": send_beside}
    steps |= {f"P{c}": functools.partial(products, c) for c in CHUNKS}
    steps |= {f"A{c}": functools.partial(send_sums, c) for c in CHUNKS}
    steps |= {f"M{c}": functools.partial(new_momentum, c) for c in CHUNKS}
    for step in ORDER:
        steps[step]()

    wait_bytes(a_in.at[0:384], xs.at[0])
    for c in CHUNKS:
        wait_bytes(c_in.at[0:384, pl.ds(STARTS[c], WIDTHS[c])], xs.at[1 + c])
        wait_bytes(sc.at[c, 0:11], sc_s.at[c])
        wait_bytes(q[c].at[0:11], q_s.at[c])
        for side in range(2):
            wait_bytes(sch.at[c, side], sch_s.at[c, side])
            wait_bytes(qh[c].at[side], qh_s.at[c, side])
    wait_bytes(u1.at[0:7], u1_s)
    wait_bytes(u2.at[0:15], u2_s)
    wait_bytes(s3.at[0:3], s3_s)
    wait_bytes(s4.at[0:7], s4_s)
    wait_bytes(upd_v, out_sem.at[0])
    wait_bytes(mo_v, out_sem.at[1])


def hand_over(upd, mo, upd_out, mo_out, upd_v, mo_v, sem):
    pairs = ((mo, mo_v, mo_out), (upd, upd_v, upd_out))
    into = [pltpu.make_async_copy(src, held, sem.at[i]) for i, (src, held, _) in enumerate(pairs)]
    out = [pltpu.make_async_copy(held, dst, sem.at[2 + i]) for i, (_, held, dst) in enumerate(pairs)]
    for copy in into:
        copy.start()
    for before, after in zip(into, out):
        before.wait()
        after.start()
    for copy in out:
        copy.wait()


def on_device(activations, cotangent, momentum, kept_index):
    hbm = pl.BlockSpec(memory_space=pl.ANY)
    dma = pltpu.SemaphoreType.DMA
    vmem = pltpu.VMEM
    n = len(WIDTHS)
    out_shape = (jax.ShapeDtypeStruct((16, 4096), bf16), jax.ShapeDtypeStruct((16, 4096), f32))
    update, momentum_out = pl.pallas_call(
        kernel,
        name="outer_step",
        out_shape=out_shape,
        in_specs=[hbm] * 4,
        out_specs=(hbm, hbm),
        scratch_shapes=[
            pltpu.SMEM((8,), jnp.int32),
            vmem((128, 256), bf16),
            vmem((256, 4096), bf16),
            vmem((16, 4096), f32),
            vmem((512, 256), bf16),
            vmem((512, 1024), bf16),
            vmem((8, 128, 128), f32),
            vmem((8, 128, 128), f32),
            vmem((16, 8, 128), f32),
            vmem((16, 8, 128), f32),
            vmem((4, 8, 128), f32),
            vmem((8, 8, 128), f32),
            [vmem((16, 16, w), f32) for w in WIDTHS],
            [vmem((16, 16, w), jnp.int16) for w in WIDTHS],
            [vmem((12, 16, w), jnp.int16) for w in WIDTHS],
            [vmem((2, 2, 16, w), jnp.int16) for w in WIDTHS],
            vmem((n, 16, 1, 128), f32),
            vmem((n, 12, 1, 128), f32),
            vmem((n, 2, 2, 1, 128), f32),
            vmem((16, 4096), bf16),
            vmem((16, 4096), f32),
            dma((7,)),
            dma((2,)),
            dma((1 + n,)),
            dma((1 + n,)),
            *[dma] * 8,
            dma((n,)),
            dma((n,)),
            dma((n, 2)),
            dma((n, 2)),
            dma((n,)),
            dma((n,)),
            dma((n, 2)),
            dma((n, 2)),
            pltpu.SemaphoreType.REGULAR((2,)),
        ],
        compiler_params=pltpu.CompilerParams(
            collective_id=1, has_side_effects=True, vmem_limit_bytes=60 * 1024 * 1024
        ),
    )(kept_index, activations[0], cotangent[0], momentum[0])
    update, momentum_out = pl.pallas_call(
        hand_over,
        name="hand_over",
        out_shape=out_shape,
        in_specs=[hbm] * 2,
        out_specs=(hbm, hbm),
        scratch_shapes=[vmem((16, 4096), bf16), vmem((16, 4096), f32), dma((4,))],
        compiler_params=pltpu.CompilerParams(vmem_limit_bytes=60 * 1024 * 1024),
    )(update, momentum_out)
    return update, momentum_out[None]


def solution(mesh):
    return jax.shard_map(
        on_device,
        mesh=mesh,
        in_specs=(
            P("replica", "fsdp", None),
            P("replica", "fsdp", None),
            P("replica", "fsdp", None),
            P(),
        ),
        out_specs=(P("fsdp", None), P("replica", "fsdp", None)),
        check_vma=False,
    )
```
